32 devices in a mesh: blk: 8 (over z, y), tp: 4 (over x, core).
Axes of the slice: x: 2, y: 2, z: 4, core: 2. Of those that a mesh axis runs over, the one named last changes fastest.
Arguments:
- tokens: bfloat16 [2048, 1536], P('blk'), may hold values from -6 to 6
- lengths: int32 [5], replicated, may hold values from 1 to 1792, as said below
- attention_gain_one: float32 [1536], replicated, may hold values from 0.25 to 1.75
- query_one: bfloat16 [1536, 1536], P(None, 'tp'), may hold values from -0.15625 to 0.15625
- first_key_matrix: bfloat16 [1536, 768], P(None, 'tp'), may hold values from -0.15625 to 0.15625
- first_value_matrix: bfloat16 [1536, 768], P(None, 'tp'), may hold values from -0.15625 to 0.15625
- projection_one: bfloat16 [1536, 1536], P('tp'), may hold values from -1.75 to 1.75
- feedforward_gain_one: float32 [1536], replicated, may hold values from 0.25 to 1.75
- gate_one: bfloat16 [1536, 4096], P(None, 'tp'), may hold values from -0.15625 to 0.15625
- up_one: bfloat16 [1536, 4096], P(None, 'tp'), may hold values from -0.15625 to 0.15625
- down_one: bfloat16 [4096, 1536], P('tp'), may hold values from -0.09375 to 0.09375
- attention_gain_two: float32 [1536], replicated, may hold values from 0.25 to 1.75
- query_two: bfloat16 [1536, 1536], P(None, 'tp'), may hold values from -0.15625 to 0.15625
- second_key_matrix: bfloat16 [1536, 768], P(None, 'tp'), may hold values from -0.15625 to 0.15625
- second_value_matrix: bfloat16 [1536, 768], P(None, 'tp'), may hold values from -0.15625 to 0.15625
- projection_two: bfloat16 [1536, 1536], P('tp'), may hold values from -1.75 to 1.75
- feedforward_gain_two: float32 [1536], replicated, may hold values from 0.25 to 1.75
- gate_two: bfloat16 [1536, 4096], P(None, 'tp'), may hold values from -0.15625 to 0.15625
- up_two: bfloat16 [1536, 4096], P(None, 'tp'), may hold values from -0.15625 to 0.15625
- down_two: bfloat16 [4096, 1536], P('tp'), may hold values from -0.09375 to 0.09375
- cotangent: bfloat16 [2048, 1536], P('blk'), may hold values from -6 to 6
Outputs:
- output: bfloat16 [2048, 1536], P('blk')
- tokens_gradient: float32 [2048, 1536], P('blk')
- gradient_attention_gain_one: float32 [1536], P('blk')
- gradient_query_one: float32 [1536, 1536], P('blk', 'tp')
- gradient_key_one: float32 [1536, 768], P('blk', 'tp')
- gradient_value_one: float32 [1536, 768], P('blk', 'tp')
- gradient_projection_one: float32 [1536, 1536], P('tp', 'blk')
- gradient_feedforward_gain_one: float32 [1536], P('blk')
- gradient_gate_one: float32 [1536, 4096], P('blk', 'tp')
- gradient_up_one: float32 [1536, 4096], P('blk', 'tp')
- gradient_down_one: float32 [4096, 1536], P('tp', 'blk')
- gradient_attention_gain_two: float32 [1536], P('blk')
- gradient_query_two: float32 [1536, 1536], P('blk', 'tp')
- gradient_key_two: float32 [1536, 768], P('blk', 'tp')
- gradient_value_two: float32 [1536, 768], P('blk', 'tp')
- gradient_projection_two: float32 [1536, 1536], P('tp', 'blk')
- gradient_feedforward_gain_two: float32 [1536], P('blk')
- gradient_gate_two: float32 [1536, 4096], P('blk', 'tp')
- gradient_up_two: float32 [1536, 4096], P('blk', 'tp')
- gradient_down_two: float32 [4096, 1536], P('tp', 'blk')
The draws below stay inside these ranges and needn't reach their ends.
Inputs may be any that keep to these rules, and one draw needn't show every extreme that they name: `lengths`: five documents in pack order; the third has exactly 1792 tokens and begins within the first 256 tokens, so it reaches from the first block of the pack to the last; the other four are shorter than 256.
All inputs are finite; a program needn't handle non-finite values.
Results may differ from the reference program's by a relative error of at most 0.034.
Values may be sent and summed in bfloat16 or wider, within the bound.
No kernel may reach another device: no remote copies, remote signals or barrier semaphores. Data moves between devices by JAX's collectives and lax.ppermute only.
A program may use at most 256 MiB of HBM per device.

```python
import math
import jax
import jax.numpy as jnp
from jax import lax

MODEL_WIDTH = 1536
QUERY_HEAD_COUNT = 16
KV_HEAD_COUNT = 8
HEAD_SIZE = 96
FF = 4096
TOK_DEV = 256
PACK_TOKENS = 2048


def draw_lengths(key, part):
    key = jax.random.fold_in(key, 11)
    first_key, second_key, third_key = jax.random.split(key, 3)
    prefix = jax.random.randint(first_key, (), 2, TOK_DEV - 1)
    head = jax.random.randint(second_key, (), 1, prefix)
    suffix = TOK_DEV - prefix
    tail = jax.random.randint(third_key, (), 1, suffix)
    middle = jnp.zeros((), jnp.int32) + (PACK_TOKENS - TOK_DEV)
    return jnp.stack([head, prefix - head, middle, tail, suffix - tail]).astype(jnp.int32)


def shard_levels(own_key, dims, cuts, low, largest):
    def one(position, parts):
        draws = jax.random.uniform(jax.random.fold_in(jax.random.fold_in(own_key, 6), position), (parts,), jnp.float32, low / len(cuts), largest / len(cuts))
        return jnp.repeat(jnp.exp(draws), dims[position] // parts).reshape((-1,) + (1,) * (len(dims) - position - 1))

    level = one(*cuts[0])
    for cut in cuts[1:]:
        level = level * one(*cut)
    return level


def noise(rng, shape, deviation, most, shards=(), kind=jnp.bfloat16):
    factor_of = shard_levels(rng, shape, shards, -0.22, 0.18) if shards else 1.0
    entries = jax.random.normal(rng, shape, jnp.float32) * deviation * factor_of
    return jnp.minimum(jnp.maximum(entries, -most), most).astype(kind)


def setup_inputs(seed: int = 0) -> dict:
    streams_of = jax.random.split(jax.random.key(seed), 22)
    tokens = noise(streams_of[0], (PACK_TOKENS, MODEL_WIDTH), 1.0, 6.0, ((0, 8),))
    lengths = draw_lengths(jax.random.fold_in(streams_of[21], 71), 0)
    attention_gain_one = jnp.clip(1.0 + 0.15 * jax.random.normal(streams_of[2], (MODEL_WIDTH,), jnp.float32), 0.25, 1.75)
    query_one = noise(streams_of[3], (MODEL_WIDTH, QUERY_HEAD_COUNT * HEAD_SIZE), MODEL_WIDTH ** -0.5, 0.15625, ((1, 4),))
    first_key_matrix = noise(streams_of[4], (MODEL_WIDTH, KV_HEAD_COUNT * HEAD_SIZE), MODEL_WIDTH ** -0.5, 0.15625, ((1, 4),))
    first_value_matrix = noise(streams_of[5], (MODEL_WIDTH, KV_HEAD_COUNT * HEAD_SIZE), MODEL_WIDTH ** -0.5, 0.15625, ((1, 4),))
    projection_one = noise(streams_of[6], (QUERY_HEAD_COUNT * HEAD_SIZE, MODEL_WIDTH), (QUERY_HEAD_COUNT * HEAD_SIZE // 128) ** -0.5, 1.75, ((0, 4),))
    feedforward_gain_one = jnp.clip(1.0 + 0.15 * jax.random.normal(streams_of[7], (MODEL_WIDTH,), jnp.float32), 0.25, 1.75)
    gate_one = noise(streams_of[8], (MODEL_WIDTH, FF), MODEL_WIDTH ** -0.5, 0.15625, ((1, 4),))
    up_one = noise(streams_of[9], (MODEL_WIDTH, FF), MODEL_WIDTH ** -0.5, 0.15625, ((1, 4),))
    down_one = noise(streams_of[10], (FF, MODEL_WIDTH), FF ** -0.5, 0.09375, ((0, 4),))
    attention_gain_two = jnp.clip(1.0 + 0.15 * jax.random.normal(streams_of[11], (MODEL_WIDTH,), jnp.float32), 0.25, 1.75)
    query_two = noise(streams_of[12], (MODEL_WIDTH, QUERY_HEAD_COUNT * HEAD_SIZE), MODEL_WIDTH ** -0.5, 0.15625, ((1, 4),))
    second_key_matrix = noise(streams_of[13], (MODEL_WIDTH, KV_HEAD_COUNT * HEAD_SIZE), MODEL_WIDTH ** -0.5, 0.15625, ((1, 4),))
    second_value_matrix = noise(streams_of[14], (MODEL_WIDTH, KV_HEAD_COUNT * HEAD_SIZE), MODEL_WIDTH ** -0.5, 0.15625, ((1, 4),))
    projection_two = noise(streams_of[15], (QUERY_HEAD_COUNT * HEAD_SIZE, MODEL_WIDTH), (QUERY_HEAD_COUNT * HEAD_SIZE // 128) ** -0.5, 1.75, ((0, 4),))
    feedforward_gain_two = jnp.clip(1.0 + 0.15 * jax.random.normal(streams_of[16], (MODEL_WIDTH,), jnp.float32), 0.25, 1.75)
    gate_two = noise(streams_of[17], (MODEL_WIDTH, FF), MODEL_WIDTH ** -0.5, 0.15625, ((1, 4),))
    up_two = noise(streams_of[18], (MODEL_WIDTH, FF), MODEL_WIDTH ** -0.5, 0.15625, ((1, 4),))
    down_two = noise(streams_of[19], (FF, MODEL_WIDTH), FF ** -0.5, 0.09375, ((0, 4),))
    cotangent = noise(streams_of[20], (PACK_TOKENS, MODEL_WIDTH), 1.0, 6.0, ((0, 8),))
    return dict(tokens=tokens, lengths=lengths, attention_gain_one=attention_gain_one, query_one=query_one, first_key_matrix=first_key_matrix, first_value_matrix=first_value_matrix, projection_one=projection_one, feedforward_gain_one=feedforward_gain_one, gate_one=gate_one, up_one=up_one, down_one=down_one, attention_gain_two=attention_gain_two, query_two=query_two, second_key_matrix=second_key_matrix, second_value_matrix=second_value_matrix, projection_two=projection_two, feedforward_gain_two=feedforward_gain_two, gate_two=gate_two, up_two=up_two, down_two=down_two, cotangent=cotangent)


PRECISION_HIGH = lax.Precision.HIGHEST
EPSILON = 1e-05
ROTARY_BASE = 100000.0
NEGATIVE = -1e+30

@jax.custom_vjp
def reduced_input(v):
    return lax.optimization_barrier(v.astype(jnp.bfloat16)).astype(jnp.float32)

@jax.custom_vjp
def reduced_gradient(v):
    return v

def low_keep(v):
    return (reduced_input(v), None)

def low_pass(kept, grad):
    return (grad,)

def back_keep(v):
    return (v, None)

def back_low(kept, grad):
    return (reduced_input(grad),)
reduced_input.defvjp(low_keep, low_pass)
reduced_gradient.defvjp(back_keep, back_low)

def rms_norm(value_rows, gain):
    return value_rows * lax.rsqrt(lax.optimization_barrier(jnp.mean(value_rows * value_rows, axis=-1, keepdims=True)) + EPSILON) * gain

def rotate(value_rows, cosine, sine):
    half = value_rows.shape[-1] // 2
    turned = jnp.concatenate([-value_rows[..., half:], value_rows[..., :half]], axis=-1)
    return value_rows * cosine + turned * sine

def rotary_tables(positions):
    half = HEAD_SIZE // 2
    rates = ROTARY_BASE ** (-(jnp.arange(half).astype(jnp.float32) * 2.0 / HEAD_SIZE))
    angle = positions.astype(jnp.float32)[:, None] * rates[None, :]
    angle = jnp.concatenate([angle, angle], axis=-1)
    return (jnp.cos(angle)[:, None, :], jnp.sin(angle)[:, None, :])

def documents(lengths, index):
    bounds = jnp.cumsum(lengths).astype(jnp.int32)
    starts = (bounds - lengths).astype(jnp.int32)
    owner = lax.optimization_barrier(jnp.sum((index[:, None] >= bounds[None, :]).astype(jnp.int32), axis=1)).astype(jnp.int32)
    picks = owner[:, None] == jnp.arange(lengths.shape[0], dtype=jnp.int32)[None, :]
    first = lax.optimization_barrier(jnp.sum(jnp.where(picks, starts[None, :], 0), axis=1)).astype(jnp.int32)
    return (owner, first)

def attend_block(query_rows, key_rows, value_rows, query_doc, key_doc, query_place, key_place):
    head_group = QUERY_HEAD_COUNT // KV_HEAD_COUNT
    token_rows = query_rows.shape[0]
    grouped_heads = query_rows.reshape(token_rows, KV_HEAD_COUNT, head_group, HEAD_SIZE)
    raw = reduced_gradient(jnp.einsum('qhgd,khd->hgqk', grouped_heads, key_rows, precision=PRECISION_HIGH))
    seen = (query_doc[:, None] == key_doc[None, :]) & (key_place[None, :] <= query_place[:, None])
    scores = jnp.where(seen, raw * HEAD_SIZE ** (-0.5), NEGATIVE)
    top = lax.optimization_barrier(jnp.max(scores, axis=-1, keepdims=True))
    weights = jnp.exp(scores - top)
    weights = weights / lax.optimization_barrier(jnp.sum(weights, axis=-1, keepdims=True))
    mixed = jnp.einsum('hgqk,khd->qhgd', reduced_input(weights), value_rows, precision=PRECISION_HIGH)
    return mixed.reshape(token_rows, QUERY_HEAD_COUNT * HEAD_SIZE)

def attention(query_rows, key_rows, value_rows, owner, index):
    size = math.gcd(PACK_TOKENS, 512)
    block = jax.checkpoint(attend_block)
    pieces = []
    for number in range(PACK_TOKENS // size):
        lo_row = number * size
        hi_row = lo_row + size
        pieces.append(block(query_rows[lo_row:hi_row], key_rows[:hi_row], value_rows[:hi_row], owner[lo_row:hi_row], owner[:hi_row], index[lo_row:hi_row], index[:hi_row]))
    return jnp.concatenate(pieces, axis=0)

def layer(inputs, cosine, sine, owner, index, attention_gain, query, key, value_matrix, projection, feedforward_gain, gate, up, down):
    normalized_input = reduced_input(rms_norm(inputs, attention_gain))
    query_rows = reduced_gradient(jnp.dot(normalized_input, query, precision=PRECISION_HIGH)).reshape(PACK_TOKENS, QUERY_HEAD_COUNT, HEAD_SIZE)
    query_rows = reduced_input(rotate(query_rows, cosine, sine))
    key_rows = reduced_gradient(jnp.dot(normalized_input, key, precision=PRECISION_HIGH)).reshape(PACK_TOKENS, KV_HEAD_COUNT, HEAD_SIZE)
    key_rows = reduced_input(rotate(key_rows, cosine, sine))
    value_rows = reduced_input(reduced_gradient(jnp.dot(normalized_input, value_matrix, precision=PRECISION_HIGH))).reshape(PACK_TOKENS, KV_HEAD_COUNT, HEAD_SIZE)
    mixed = attention(query_rows, key_rows, value_rows, owner, index)
    mixed = reduced_input(reduced_gradient(mixed))
    hidden = inputs + reduced_gradient(jnp.dot(mixed, projection, precision=PRECISION_HIGH))
    inner_in = reduced_input(rms_norm(hidden, feedforward_gain))
    gate_out = reduced_gradient(jnp.dot(inner_in, gate, precision=PRECISION_HIGH))
    up_out = reduced_gradient(jnp.dot(inner_in, up, precision=PRECISION_HIGH))
    inner = reduced_input(jax.nn.silu(gate_out) * up_out)
    return hidden + reduced_gradient(jnp.dot(inner, down, precision=PRECISION_HIGH))

def reference(tokens, lengths, attention_gain_one, query_one, first_key_matrix, first_value_matrix, projection_one, feedforward_gain_one, gate_one, up_one, down_one, attention_gain_two, query_two, second_key_matrix, second_value_matrix, projection_two, feedforward_gain_two, gate_two, up_two, down_two, cotangent):
    index = jnp.arange(PACK_TOKENS, dtype=jnp.int32)
    owner, first = documents(lengths, index)
    cosine, sine = rotary_tables(index - first)
    weights = [attention_gain_one, query_one, first_key_matrix, first_value_matrix, projection_one, feedforward_gain_one, gate_one, up_one, down_one, attention_gain_two, query_two, second_key_matrix, second_value_matrix, projection_two, feedforward_gain_two, gate_two, up_two, down_two]
    weights = [w.astype(jnp.float32) for w in weights]

    def forward(inputs, *params):
        middle = layer(inputs, cosine, sine, owner, index, *params[:9])
        return layer(middle, cosine, sine, owner, index, *params[9:])
    result, pull = jax.vjp(forward, tokens.astype(jnp.float32), *weights)
    grads = pull(cotangent.astype(jnp.float32))
    return (result.astype(jnp.bfloat16), grads[0], grads[1], grads[2], grads[3], grads[4], grads[5], grads[6], grads[7], grads[8], grads[9], grads[10], grads[11], grads[12], grads[13], grads[14], grads[15], grads[16], grads[17], grads[18])
```

```python
import functools

import jax
import jax.numpy as jnp
from jax import lax
from jax.experimental import pallas as pl
from jax.experimental.pallas import tpu as pltpu
from jax.sharding import PartitionSpec as P

HEAD_SIZE = 96
EPSILON = 1e-05
ROTARY_BASE = 100000.0
NEGATIVE = -1e30
SCALE = HEAD_SIZE ** (-0.5)
BF16 = jnp.bfloat16
F32 = jnp.float32


def product(left, right):
    return jnp.dot(left, right, preferred_element_type=F32)


def product_left(left, right):
    return lax.dot_general(left, right, (((0,), (0,)), ((), ())), preferred_element_type=F32)


def product_right(left, right):
    return lax.dot_general(left, right, (((1,), (1,)), ((), ())), preferred_element_type=F32)


def rms_norm(rows, gain):
    return rows * lax.rsqrt(jnp.mean(rows * rows, axis=-1, keepdims=True) + EPSILON) * gain


def rms_norm_back(rows, gain, incoming):
    scale = lax.rsqrt(jnp.mean(rows * rows, axis=-1, keepdims=True) + EPSILON)
    weighted = incoming * gain
    inner = jnp.mean(rows * weighted, axis=-1, keepdims=True)
    back = scale * weighted - rows * (scale * scale * scale * inner)
    return back, jnp.sum(incoming * rows * scale, axis=0)


def rotate(rows, cosine, sine):
    half = HEAD_SIZE // 2
    turned = jnp.concatenate([-rows[..., half:], rows[..., :half]], axis=-1)
    return rows * cosine + turned * sine


def unrotate(rows, cosine, sine):
    half = HEAD_SIZE // 2
    scaled = rows * sine
    return rows * cosine + jnp.concatenate([scaled[..., half:], -scaled[..., :half]], axis=-1)


def rotary_tables(positions):
    half = HEAD_SIZE // 2
    rates = ROTARY_BASE ** (-(jnp.arange(half).astype(F32) * 2.0 / HEAD_SIZE))
    angle = positions.astype(F32)[:, None] * rates[None, :]
    angle = jnp.concatenate([angle, angle], axis=-1)
    return jnp.cos(angle), jnp.sin(angle)


def first_tokens(lengths, index):
    bounds = jnp.cumsum(lengths)
    starts = bounds - lengths
    owner = jnp.sum((index[:, None] >= bounds[None, :]).astype(jnp.int32), axis=1)
    picks = owner[:, None] == jnp.arange(lengths.shape[0], dtype=jnp.int32)[None, :]
    return jnp.sum(jnp.where(picks, starts[None, :], 0), axis=1).astype(jnp.int32)


def swap(rows, axis, size, bit):
    return lax.ppermute(rows, axis, [(i, i ^ bit) for i in range(size)])


def sum_tp(partial, core):
    half = partial.shape[0] // 2
    keep = lax.dynamic_slice_in_dim(partial, core * half, half, 0)
    give = lax.dynamic_slice_in_dim(partial, (1 - core) * half, half, 0).astype(BF16)
    pair = (keep + swap(give, "tp", 4, 1).astype(F32)).astype(BF16)
    whole = (pair.astype(F32) + swap(pair, "tp", 4, 2).astype(F32)).astype(BF16)
    other = swap(whole, "tp", 4, 1)
    top = jnp.where(core == 0, whole, other)
    bottom = jnp.where(core == 0, other, whole)
    return jnp.concatenate([top, bottom], axis=0)


def line_gather(rows, blocks, step):
    slots = [rows, swap(rows, "blk", blocks, 1)]
    current = rows
    for _ in range(blocks // 2 - 1):
        pairs = [(i, i + step) for i in range(blocks) if 0 <= i + step < blocks]
        current = lax.ppermute(current, "blk", pairs)
        slots += [current, swap(current, "blk", blocks, 1)]
    return slots


def gather_rows(rows, core):
    half = rows.shape[0] // 2
    own = lax.all_gather(
        lax.dynamic_slice_in_dim(rows, core * half, half, 0), "blk", axis=0, tiled=True
    )
    return own, swap(own, "tp", 4, 1)


WHOLE = pl.BlockSpec(memory_space=pltpu.VMEM)
SCALARS = pl.BlockSpec(memory_space=pltpu.SMEM)


def head_rows(ref, head, group, tokens):
    parts = []
    for member in range(group):
        lane = (head * group + member) * HEAD_SIZE
        parts.append(ref[:tokens, lane : lane + HEAD_SIZE])
    return jnp.concatenate(parts, axis=0)


def wide(row, group):
    return jnp.concatenate([row] * group, axis=1)


def seen_mask(first_row, key_start, query_start, tokens, group):
    shape = (tokens, tokens)
    key = key_start + lax.broadcasted_iota(jnp.int32, shape, 0)
    query = query_start + lax.broadcasted_iota(jnp.int32, shape, 1)
    seen = (key <= query) & (key >= first_row)
    return jnp.concatenate([seen.astype(F32)] * group, axis=1) > 0.5


def earlier_block(own, slot):
    place = own // 2 - slot // 2
    block = place * 2 + jnp.bitwise_xor(lax.rem(own, 2), slot % 2)
    return block, (place >= 0) & (block <= own)


def later_block(own, slot, blocks):
    place = own // 2 + slot // 2
    block = place * 2 + jnp.bitwise_xor(lax.rem(own, 2), slot % 2)
    return block, (place < blocks // 2) & (block >= own)


def attend_kernel(blocks, heads, group, scalars, firsts, query, *refs):
    pairs = refs[:blocks]
    mixed_ref, log_ref, scores, top, total = refs[blocks:]
    tokens = query.shape[0]
    own = scalars[0]
    first_row = firsts[pl.ds(own, 1), :]
    for head in range(heads):
        rows = head_rows(query, head, group, tokens)
        top[...] = jnp.full_like(top, NEGATIVE)
        for slot in range(blocks):
            block, valid = earlier_block(own, slot)

            @pl.when(valid)
            def _():
                keys = pairs[slot][:, head * HEAD_SIZE : (head + 1) * HEAD_SIZE]
                found = product_right(keys, rows) * SCALE
                seen = seen_mask(first_row, block * tokens, own * tokens, tokens, group)
                found = jnp.where(seen, found, NEGATIVE)
                scores[slot] = found
                top[...] = jnp.maximum(top[...], jnp.max(found, axis=0, keepdims=True))

        highest = top[0:1, :]
        total[...] = jnp.zeros_like(total)
        top[...] = jnp.zeros_like(top)
        for slot in range(blocks):
            block, valid = earlier_block(own, slot)

            @pl.when(valid)
            def _():
                lane = (heads + head) * HEAD_SIZE
                values = pairs[slot][:, lane : lane + HEAD_SIZE]
                weights = jnp.exp(scores[slot] - highest)
                top[...] += jnp.sum(weights, axis=0, keepdims=True)
                total[...] += product_left(values, weights.astype(BF16))

        mass = top[0:1, :]
        result = (total[...] / mass).T
        logs = highest + jnp.log(mass)
        for member in range(group):
            lane = (head * group + member) * HEAD_SIZE
            part = slice(member * tokens, (member + 1) * tokens)
            mixed_ref[:, lane : lane + HEAD_SIZE] = result[part].astype(BF16)
            log_ref[head * group + member : head * group + member + 1, :] = logs[:, part]


def attend(query, pairs, firsts, own, heads, group):
    tokens, width = query.shape
    blocks = len(pairs)
    return pl.pallas_call(
        functools.partial(attend_kernel, blocks, heads, group),
        out_shape=(
            jax.ShapeDtypeStruct((tokens, width), BF16),
            jax.ShapeDtypeStruct((heads * group, tokens), F32),
        ),
        in_specs=[SCALARS] + [WHOLE] * (2 + blocks),
        out_specs=(WHOLE, WHOLE),
        scratch_shapes=[
            pltpu.VMEM((blocks, tokens, group * tokens), F32),
            pltpu.VMEM((8, group * tokens), F32),
            pltpu.VMEM((HEAD_SIZE, group * tokens), F32),
        ],
        compiler_params=pltpu.CompilerParams(vmem_limit_bytes=48 * 1024 * 1024),
        name="attend",
    )(own.reshape(1), firsts, query, *pairs)


def query_back_kernel(
    blocks, heads, group, scalars, firsts, query, back, logs, delta, cosine, sine, *refs
):
    pairs = refs[:blocks]
    out_ref, total = refs[blocks:]
    tokens = query.shape[0]
    own = scalars[0]
    first_row = firsts[pl.ds(own, 1), :]
    for head in range(heads):
        rows = head_rows(query, head, group, tokens)
        back_rows = head_rows(back, head, group, tokens)
        members = range(head * group, (head + 1) * group)
        log_row = jnp.concatenate([logs[m : m + 1, :] for m in members], axis=1)
        delta_row = jnp.concatenate([delta[m : m + 1, :] for m in members], axis=1)
        total[...] = jnp.zeros_like(total)
        for slot in range(blocks):
            block, valid = earlier_block(own, slot)

            @pl.when(valid)
            def _():
                lane = head * HEAD_SIZE
                keys = pairs[slot][:, lane : lane + HEAD_SIZE]
                lane = (heads + head) * HEAD_SIZE
                values = pairs[slot][:, lane : lane + HEAD_SIZE]
                found = product_right(keys, rows) * SCALE - log_row
                seen = seen_mask(first_row, block * tokens, own * tokens, tokens, group)
                probs = jnp.exp(jnp.where(seen, found, NEGATIVE))
                back_probs = product_right(values, back_rows)
                back_scores = (probs * (back_probs - delta_row) * SCALE).astype(BF16)
                total[...] += product_left(keys, back_scores)

        result = total[...].T
        for member in range(group):
            lane = (head * group + member) * HEAD_SIZE
            part = result[member * tokens : (member + 1) * tokens]
            out_ref[:, lane : lane + HEAD_SIZE] = unrotate(part, cosine[...], sine[...]).astype(
                BF16
            )


def query_back(query, back, logs, delta, pairs, firsts, own, tables, heads, group):
    tokens, width = query.shape
    blocks = len(pairs)
    return pl.pallas_call(
        functools.partial(query_back_kernel, blocks, heads, group),
        out_shape=jax.ShapeDtypeStruct((tokens, width), BF16),
        in_specs=[SCALARS] + [WHOLE] * (7 + blocks),
        out_specs=WHOLE,
        scratch_shapes=[pltpu.VMEM((HEAD_SIZE, group * tokens), F32)],
        compiler_params=pltpu.CompilerParams(vmem_limit_bytes=48 * 1024 * 1024),
        name="query_back",
    )(own.reshape(1), firsts, query, back, logs, delta, *tables, *pairs)


def split_rows(rows):
    high = rows.astype(BF16)
    return high, (rows - high.astype(F32)).astype(BF16)


def pack_rows(rows, extra):
    high, low = split_rows(extra)
    count, tokens = extra.shape
    both = jnp.concatenate([high, low], axis=0)
    both = jnp.pad(both, ((0, 16 - 2 * count), (0, rows.shape[1] - tokens)))
    return jnp.concatenate([rows, both], axis=0)


def pair_back_kernel(blocks, heads, group, scalars, firsts, pairs, cosine, sine, *refs):
    queries, backs = refs[:blocks], refs[blocks : 2 * blocks]
    out_ref, key_total, value_total = refs[2 * blocks :]
    tokens = pairs.shape[0]
    own = scalars[0]
    count = heads * group
    for head in range(heads):
        lane = head * HEAD_SIZE
        keys = pairs[:, lane : lane + HEAD_SIZE]
        value_lane = (heads + head) * HEAD_SIZE
        values = pairs[:, value_lane : value_lane + HEAD_SIZE]
        key_total[...] = jnp.zeros_like(key_total)
        value_total[...] = jnp.zeros_like(value_total)
        for slot in range(blocks):
            block, valid = later_block(own, slot, blocks)

            @pl.when(valid)
            def _():
                rows = head_rows(queries[slot], head, group, tokens)
                back_rows = head_rows(backs[slot], head, group, tokens)

                def extra(ref):
                    below = ref[tokens : tokens + 16, :tokens].astype(F32)
                    return jnp.concatenate(
                        [
                            below[m : m + 1, :] + below[count + m : count + m + 1, :]
                            for m in range(head * group, (head + 1) * group)
                        ],
                        axis=1,
                    )

                log_row = extra(queries[slot])
                delta_row = extra(backs[slot])
                first_row = firsts[pl.ds(block, 1), :]
                found = product_right(keys, rows) * SCALE - log_row
                seen = seen_mask(first_row, own * tokens, block * tokens, tokens, group)
                probs = jnp.exp(jnp.where(seen, found, NEGATIVE))
                back_probs = product_right(values, back_rows)
                back_scores = (probs * (back_probs - delta_row) * SCALE).astype(BF16)
                key_total[...] += product(back_scores, rows)
                value_total[...] += product(probs.astype(BF16), back_rows)

        out_ref[:, lane : lane + HEAD_SIZE] = unrotate(
            key_total[...], cosine[...], sine[...]
        ).astype(BF16)
        out_ref[:, value_lane : value_lane + HEAD_SIZE] = value_total[...].astype(BF16)


def pair_back(pairs, queries, backs, firsts, own, tables, heads, group):
    tokens, width = pairs.shape
    blocks = len(queries)
    return pl.pallas_call(
        functools.partial(pair_back_kernel, blocks, heads, group),
        out_shape=jax.ShapeDtypeStruct((tokens, width), BF16),
        in_specs=[SCALARS] + [WHOLE] * (4 + 2 * blocks),
        out_specs=WHOLE,
        scratch_shapes=[pltpu.VMEM((tokens, HEAD_SIZE), F32)] * 2,
        compiler_params=pltpu.CompilerParams(vmem_limit_bytes=48 * 1024 * 1024),
        name="pair_back",
    )(own.reshape(1), firsts, pairs, *tables, *queries, *backs)


def feedforward_weights_kernel(
    started, rows, incoming, rows_part, incoming_part, gate_weight, up_weight, down_weight, *refs
):
    before = refs[:3] if started else None
    gate_out, up_out, down_out = refs[-3:]

    @pl.when(pl.program_id(0) == 0)
    def _():
        if started:
            gate_out[...] = before[0][...]
            up_out[...] = before[1][...]
            down_out[...] = before[2][...]
        else:
            gate_out[...] = jnp.zeros_like(gate_out)
            up_out[...] = jnp.zeros_like(up_out)
            down_out[...] = jnp.zeros_like(down_out)

    gate = product(rows[...], gate_weight[...])
    up = product(rows[...], up_weight[...])
    back_inner = product_right(incoming[...], down_weight[...])
    inner, back_gate, back_up = swiglu_back(gate, up, back_inner)
    gate_out[...] += product_left(rows_part[...], back_gate)
    up_out[...] += product_left(rows_part[...], back_up)
    down_out[...] += product_left(inner, incoming_part[...])


def feedforward_weights(rows, incoming, place, blocks, weights, before=None):
    gate_weight, up_weight, down_weight = weights
    total, width = rows.shape
    hidden = gate_weight.shape[1]
    part = width // blocks
    rows_part = lax.dynamic_slice_in_dim(rows, place * part, part, 1)
    incoming_part = lax.dynamic_slice_in_dim(incoming, place * part, part, 1)
    step = 256
    once = pl.Buffered(1)
    fixed = lambda shape: pl.BlockSpec(shape, lambda i: (0, 0), pipeline_mode=once)
    moving = lambda columns: pl.BlockSpec((step, columns), lambda i: (i, 0))
    shapes = [(part, hidden), (part, hidden), (hidden, part)]
    started = before is not None
    return pl.pallas_call(
        functools.partial(feedforward_weights_kernel, started),
        grid=(total // step,),
        out_shape=tuple(jax.ShapeDtypeStruct(shape, F32) for shape in shapes),
        in_specs=[
            moving(width),
            moving(width),
            moving(part),
            moving(part),
            fixed((width, hidden)),
            fixed((width, hidden)),
            fixed((hidden, width)),
        ]
        + ([fixed(shape) for shape in shapes] if started else []),
        out_specs=tuple(fixed(shape) for shape in shapes),
        compiler_params=pltpu.CompilerParams(vmem_limit_bytes=48 * 1024 * 1024),
        cost_estimate=pl.CostEstimate(
            flops=6 * total * width * hidden, bytes_accessed=16000000, transcendentals=0
        ),
        name="feedforward_weights",
    )(
        rows,
        incoming,
        rows_part,
        incoming_part,
        gate_weight,
        up_weight,
        down_weight,
        *(before if started else ()),
    )


def swiglu_back(gate, up, back_inner):
    chance = 1.0 / (1.0 + jnp.exp(-gate))
    silu = gate * chance
    inner = (silu * up).astype(BF16)
    back_gate = (back_inner * up * (chance + silu * (1.0 - chance))).astype(BF16)
    back_up = (back_inner * silu).astype(BF16)
    return inner, back_gate, back_up


class Layout:
    def __init__(self, lengths, tokens):
        self.tokens = tokens
        self.blocks = lax.axis_size("blk")
        self.own = lax.axis_index("blk")
        self.core = lax.rem(lax.axis_index("tp"), 2)
        index = jnp.arange(tokens * self.blocks, dtype=jnp.int32)
        firsts = first_tokens(lengths, index)
        mine = lax.dynamic_slice_in_dim(index - firsts, self.own * tokens, tokens, 0)
        self.tables = rotary_tables(mine)
        self.firsts = firsts.reshape(self.blocks, tokens)


def attention_front(inputs, weights, layout):
    gain, query_weight, key_weight, value_weight, projection = weights[:5]
    tokens = layout.tokens
    heads = key_weight.shape[1] // HEAD_SIZE
    group = query_weight.shape[1] // HEAD_SIZE // heads
    cosine, sine = (table[:, None, :] for table in layout.tables)
    normed = rms_norm(inputs, gain).astype(BF16)

    def turned(weight):
        rows = product(normed, weight).reshape(tokens, -1, HEAD_SIZE)
        return rotate(rows, cosine, sine).astype(BF16).reshape(tokens, -1)

    query = turned(query_weight)
    pair = jnp.concatenate(
        [turned(key_weight), product(normed, value_weight).astype(BF16)], axis=1
    )
    pairs = line_gather(pair, layout.blocks, 2)
    mixed, logs = attend(query, pairs, layout.firsts, layout.own, heads, group)
    hidden = inputs + sum_tp(product(mixed, projection), layout.core).astype(F32)
    queries = line_gather(pack_rows(query, logs), layout.blocks, -2)
    return hidden, (normed, query, pairs, logs, mixed, queries, heads, group)


def feedforward_parts(inner_in, weights):
    gate = product(inner_in, weights[6])
    up = product(inner_in, weights[7])
    return gate, up


def attention_back(inputs, hidden, incoming, back_in, weights, layout, saved):
    gain, query_weight, key_weight, value_weight, projection = weights[:5]
    normed, query, pairs, logs, mixed, queries, heads, group = saved
    tokens = layout.tokens
    back_norm, gradient_feedforward_gain = rms_norm_back(hidden, weights[5], back_in)
    back_hidden = incoming + back_norm
    low = back_hidden.astype(BF16)
    back_mixed = product_right(low, projection).astype(BF16)
    delta = jnp.sum(
        (back_mixed.astype(F32) * mixed.astype(F32)).reshape(tokens, -1, HEAD_SIZE), axis=-1
    ).T
    backs = line_gather(pack_rows(back_mixed, delta), layout.blocks, -2)
    back_query = query_back(
        query, back_mixed, logs, delta, pairs, layout.firsts, layout.own, layout.tables, heads, group
    )
    back_pair = pair_back(
        pairs[0], queries, backs, layout.firsts, layout.own, layout.tables, heads, group
    )
    width = heads * HEAD_SIZE
    partial = (
        product_right(back_query, query_weight)
        + product_right(back_pair[:, :width], key_weight)
        + product_right(back_pair[:, width:], value_weight)
    )
    back_normed = sum_tp(partial, layout.core).astype(F32)
    back_inputs, gradient_attention_gain = rms_norm_back(inputs, gain, back_normed)
    back_all = jnp.concatenate([back_query, back_pair], axis=1)
    gradient_attention = product_left(normed, back_all).astype(BF16)
    gradient_projection = product_left(low, mixed).astype(BF16)
    share = lax.psum_scatter(
        jnp.concatenate([gradient_attention, gradient_projection], axis=1),
        "blk",
        scatter_dimension=0,
        tiled=True,
    ).astype(F32)
    ends = [0]
    for part in (query_weight.shape[1], width, width, query_weight.shape[1]):
        ends.append(ends[-1] + part)
    pieces = [share[:, ends[i] : ends[i + 1]] for i in range(4)]
    pieces[3] = pieces[3].T
    return (
        back_inputs + back_hidden,
        tuple(pieces),
        (gradient_attention_gain, gradient_feedforward_gain),
    )


def feedforward_share(own_rows, own_incoming, weights, layout):
    gradients = None
    for rows, incoming in zip(own_rows, own_incoming):
        gradients = feedforward_weights(
            rows, incoming, layout.own, layout.blocks, weights[6:9], gradients
        )
    return gradients


def body(tokens, lengths, *rest):
    first, second, cotangent = rest[:9], rest[9:18], rest[18]
    layout = Layout(lengths, tokens.shape[0])
    core = layout.core
    cotangents = gather_rows(cotangent, core)
    inputs_one = tokens.astype(F32)
    hidden_one, saved_one = attention_front(inputs_one, first, layout)
    inner_in_one = rms_norm(hidden_one, first[5]).astype(BF16)
    gate, up = feedforward_parts(inner_in_one, first)
    inner = (jax.nn.silu(gate) * up).astype(BF16)
    inputs_two = hidden_one + sum_tp(product(inner, first[8]), core).astype(F32)
    inner_ins_one = gather_rows(inner_in_one, core)
    hidden_two, saved_two = attention_front(inputs_two, second, layout)
    inner_in_two = rms_norm(hidden_two, second[5]).astype(BF16)
    inner_ins_two = gather_rows(inner_in_two, core)

    def back_feedforward(inner_in, incoming, weights, forward):
        gate, up = feedforward_parts(inner_in, weights)
        back_inner = product_right(incoming, weights[8])
        inner, back_gate, back_up = swiglu_back(gate, up, back_inner)
        partial = product_right(back_gate, weights[6]) + product_right(back_up, weights[7])
        back_in = sum_tp(partial, core).astype(F32)
        if not forward:
            return back_in, None
        return back_in, sum_tp(product(inner, weights[8]), core).astype(F32)

    back_in, last = back_feedforward(inner_in_two, cotangent, second, True)
    result = (hidden_two + last).astype(BF16)
    back_two, shares_two, gains_two = attention_back(
        inputs_two, hidden_two, cotangent.astype(F32), back_in, second, layout, saved_two
    )
    low_two = back_two.astype(BF16)
    lows = gather_rows(low_two, core)
    back_in, _ = back_feedforward(inner_in_one, low_two, first, False)
    back_one, shares_one, gains_one = attention_back(
        inputs_one, hidden_one, back_two, back_in, first, layout, saved_one
    )
    feed_two = feedforward_share(inner_ins_two, cotangents, second, layout)
    feed_one = feedforward_share(inner_ins_one, lows, first, layout)
    gains = jnp.stack([gains_one[0], gains_one[1], gains_two[0], gains_two[1]], axis=0)
    gains = gains.reshape(4, layout.blocks, -1).transpose(1, 0, 2)
    gains = jnp.sum(lax.all_to_all(gains, "blk", 0, 0, tiled=True), axis=0)
    return (
        (result, back_one)
        + (gains[0],)
        + shares_one
        + (gains[1],)
        + feed_one
        + (gains[2],)
        + shares_two
        + (gains[3],)
        + feed_two
    )


def solution(mesh):
    rows, columns = P("tp", None), P(None, "tp")
    layer = (P(), columns, columns, columns, rows, P(), columns, columns, rows)
    in_specs = (P("blk", None), P()) + layer + layer + (P("blk", None),)
    wide_out, tall_out = P("blk", "tp"), P("tp", "blk")
    layer_out = (
        P("blk"),
        wide_out,
        wide_out,
        wide_out,
        tall_out,
        P("blk"),
        wide_out,
        wide_out,
        tall_out,
    )
    out_specs = (P("blk", None), P("blk", None)) + layer_out + layer_out
    return jax.shard_map(body, mesh=mesh, in_specs=in_specs, out_specs=out_specs, check_vma=False)
```

```python
import functools

import jax
import jax.numpy as jnp
from jax import lax
from jax.experimental import pallas as pl
from jax.experimental.pallas import tpu as pltpu
from jax.sharding import PartitionSpec as P

HEAD_SIZE = 96
EPSILON = 1e-05
ROTARY_BASE = 100000.0
NEGATIVE = -1e30
SCALE = HEAD_SIZE ** (-0.5)
BF16 = jnp.bfloat16
F32 = jnp.float32


def product(left, right):
    return jnp.dot(left, right, preferred_element_type=F32)


def product_left(left, right):
    return lax.dot_general(left, right, (((0,), (0,)), ((), ())), preferred_element_type=F32)


def product_right(left, right):
    return lax.dot_general(left, right, (((1,), (1,)), ((), ())), preferred_element_type=F32)


def rms_norm(rows, gain):
    return rows * lax.rsqrt(jnp.mean(rows * rows, axis=-1, keepdims=True) + EPSILON) * gain


def rms_norm_back(rows, gain, incoming):
    scale = lax.rsqrt(jnp.mean(rows * rows, axis=-1, keepdims=True) + EPSILON)
    weighted = incoming * gain
    inner = jnp.mean(rows * weighted, axis=-1, keepdims=True)
    back = scale * weighted - rows * (scale * scale * scale * inner)
    return back, jnp.sum(incoming * rows * scale, axis=0, keepdims=True)


def rotate(rows, cosine, sine):
    half = HEAD_SIZE // 2
    turned = jnp.concatenate([-rows[..., half:], rows[..., :half]], axis=-1)
    return rows * cosine + turned * sine


def unrotate(rows, cosine, sine):
    half = HEAD_SIZE // 2
    scaled = rows * sine
    return rows * cosine + jnp.concatenate([scaled[..., half:], -scaled[..., :half]], axis=-1)


def rotary_tables(positions):
    half = HEAD_SIZE // 2
    rates = ROTARY_BASE ** (-(jnp.arange(half).astype(F32) * 2.0 / HEAD_SIZE))
    angle = positions.astype(F32)[:, None] * rates[None, :]
    angle = jnp.concatenate([angle, angle], axis=-1)
    return jnp.cos(angle), jnp.sin(angle)


def first_tokens(lengths, index):
    bounds = jnp.cumsum(lengths)
    starts = bounds - lengths
    owner = jnp.sum((index[:, None] >= bounds[None, :]).astype(jnp.int32), axis=1)
    picks = owner[:, None] == jnp.arange(lengths.shape[0], dtype=jnp.int32)[None, :]
    return jnp.sum(jnp.where(picks, starts[None, :], 0), axis=1).astype(jnp.int32)


def swap(rows, axis, size, bit):
    return lax.ppermute(rows, axis, [(i, i ^ bit) for i in range(size)])


def tie(*values):
    return lax.optimization_barrier(values)


def sum_tp(send, keep, beside=None):
    pair = (keep + swap(send, "tp", 4, 1).astype(F32)).astype(BF16)
    moved = swap(pair, "tp", 4, 2)
    done = None
    if beside is not None:
        moved, done = tie(moved, beside(pair))
    whole = (pair.astype(F32) + moved.astype(F32)).astype(BF16)
    pieces = whole, swap(whole, "tp", 4, 1)
    return pieces if beside is None else (pieces, done)


def slot_block(own, slot):
    return (own // 2 - slot // 2) * 2 + own % 2 + slot % 2 * (1 - 2 * (own % 2))


def gather_pairs(rows, blocks):
    slots = []
    for far in range(blocks // 2):
        pairs = [(i, i + 2 * far) for i in range(blocks - 2 * far)]
        slots.append(lax.ppermute(rows, "blk", pairs) if far else rows)
    return [part for near in slots for part in (near, swap(near, "blk", blocks, 1))]


def send_back(even, odd, first, blocks):
    other = swap(odd, "blk", blocks, 1)
    rows = even[0].shape[0]
    received = []
    for index, term in enumerate(even):
        theirs = other[index * rows : (index + 1) * rows]
        both = (term.astype(F32) + theirs.astype(F32)).astype(BF16)
        far = first // 2 + index
        pairs = [(i, i - 2 * far) for i in range(2 * far, blocks)]
        received.append(lax.ppermute(both, "blk", pairs) if far else both)
    return received


def sum_blocks(partial, blocks):
    rows, columns = partial.shape
    parts = lax.all_to_all(partial, "blk", 0, 0, tiled=True).reshape(blocks, -1, columns)
    return jnp.sum(parts.astype(F32), axis=0)


def sum_pair(keep, send, blocks):
    return (keep.astype(F32) + swap(send, "blk", blocks, 1).astype(F32)).astype(BF16)


def scatter_blocks(both, blocks):
    groups = [list(range(parity, blocks, 2)) for parity in range(2)]
    return lax.psum_scatter(
        both, "blk", scatter_dimension=0, axis_index_groups=groups, tiled=True
    )


def gather_rows(half):
    own = lax.all_gather(half, "blk", axis=0, tiled=True)
    return own, swap(own, "tp", 4, 1)


WHOLE = pl.BlockSpec(memory_space=pltpu.VMEM)
SCALARS = pl.BlockSpec(memory_space=pltpu.SMEM)
MEGA = 1024 * 1024
TIMES = dict(
    front=2.5,
    attend=8,
    feed_forward=7,
    feed_both=9,
    feed_back=12,
    middle_back=2.5,
    attend_back=6,
    pair_back=2,
    inputs_back=3,
    feedforward_prepare=11,
    feedforward_weights=17.5,
    feedforward_finish=10.5,
    attention_weights=2.5,
    split_share=1,
)


def cost(name):
    return pl.CostEstimate(
        flops=int(TIMES[name] * TIME_FLOPS), bytes_accessed=0, transcendentals=0
    )


TIME_FLOPS = 1.1e9


def shaped(*shapes):
    return tuple(jax.ShapeDtypeStruct(shape, kind) for shape, kind in shapes)


def call(kernel, name, info, arrays, outs, scratch=(), limit=32, **more):
    more.setdefault("in_specs", [SCALARS] + [WHOLE] * len(arrays))
    more.setdefault("out_specs", (WHOLE,) * len(outs))
    return pl.pallas_call(
        kernel,
        out_shape=shaped(*outs),
        scratch_shapes=list(scratch),
        compiler_params=pltpu.CompilerParams(vmem_limit_bytes=limit * MEGA),
        cost_estimate=cost(name),
        name=name,
        **more,
    )(info, *arrays)


def halves(info, half):
    start = pl.multiple_of(info[1] * half, half)
    return pl.ds(start, half), pl.ds(pl.multiple_of(half - start, half), half)


def join(info, pieces, put):
    whole, other = pieces
    mine, theirs = halves(info, whole.shape[0])
    put(mine, whole[...].astype(F32))
    put(theirs, other[...].astype(F32))


def part(info, total, send, keep):
    mine, theirs = halves(info, keep.shape[0])
    keep[...] = total[mine, :]
    send[...] = total[theirs, :].astype(BF16)


def both_halves(tokens, width):
    return ((tokens // 2, width), BF16), ((tokens // 2, width), F32)


def front_kernel(joined, info, base, *refs):
    if joined:
        whole, other = refs[:2]
        refs = refs[2:]
    gain, query_weight, key_weight, value_weight, cosine, sine = refs[:6]
    normed, query, pair = refs[6:9]
    if joined:
        inputs = refs[9]

        def put(rows, values):
            inputs[rows, :] = base[rows, :] + values

        join(info, (whole, other), put)
        source = inputs[...]
    else:
        source = base[...].astype(F32)
    normed[...] = rms_norm(source, gain[...]).astype(BF16)

    def turned(weight, out):
        rows = product(normed[...], weight[...])
        for lane in range(0, weight.shape[1], HEAD_SIZE):
            piece = rows[:, lane : lane + HEAD_SIZE]
            out[:, lane : lane + HEAD_SIZE] = rotate(piece, cosine[...], sine[...]).astype(BF16)

    turned(key_weight, pair)
    pair[:, key_weight.shape[1] :] = product(normed[...], value_weight[...]).astype(BF16)
    turned(query_weight, query)


def front(base, pieces, weights, layout):
    tokens, width = base.shape
    wide, narrow = weights[1].shape[1], weights[2].shape[1]
    joined = pieces is not None
    arrays = (base,) + (pieces if joined else ()) + (weights[0].reshape(1, -1),)
    arrays += tuple(weights[1:4]) + layout.tables
    outs = [((tokens, width), BF16), ((tokens, wide), BF16), ((tokens, 2 * narrow), BF16)]
    if joined:
        outs.append(((tokens, width), F32))
    return call(functools.partial(front_kernel, joined), "front", layout.info, arrays, outs)


def feed_specs(arrays, weights, chunk):
    width = weights[0].shape[0]
    across = pl.BlockSpec((width, chunk), lambda i: (0, i))
    down = pl.BlockSpec((chunk, width), lambda i: (i, 0))
    return [SCALARS] + [fixed(array.shape) for array in arrays] + [across, across, down]


def feed_call(kernel, name, layout, arrays, weights, outs, scratch):
    chunk = 256
    return call(
        kernel,
        name,
        layout.info,
        tuple(arrays) + tuple(weights),
        outs,
        scratch,
        limit=40,
        grid=(weights[0].shape[1] // chunk,),
        in_specs=feed_specs(arrays, weights, chunk),
        out_specs=tuple(fixed(shape) for shape, _ in outs),
    )


def feed_start(info, base, pieces, gain, hidden, inner_in, half):
    def put(rows, values):
        hidden[rows, :] = base[rows, :].astype(F32) + values

    join(info, pieces, put)
    inner_in[...] = rms_norm(hidden[...], gain[...]).astype(BF16)
    half[...] = inner_in[halves(info, half.shape[0])[0], :]


def feed_forward_kernel(
    info, base, whole, other, gain, beside, gate_weight, up_weight, down_weight, *refs
):
    hidden, inner_in, half, send, keep, total = refs

    @pl.when(pl.program_id(0) == 0)
    def _():
        width = base.shape[1]
        feed_start(info, base, (whole, other), gain, hidden, inner_in, half.at[:, :width])
        half[:, width:] = beside[halves(info, half.shape[0])[0], :]
        total[...] = jnp.zeros_like(total)

    gate = product(inner_in[...], gate_weight[...])
    up = product(inner_in[...], up_weight[...])
    inner = (gate / (1.0 + jnp.exp(-gate)) * up).astype(BF16)
    total[...] += product(inner, down_weight[...])

    @pl.when(pl.program_id(0) == pl.num_programs(0) - 1)
    def _():
        part(info, total, send, keep)


def feed_forward(base, pieces, beside, weights, layout):
    tokens, width = base.shape
    outs = [((tokens, width), F32), ((tokens, width), BF16), ((tokens // 2, 2 * width), BF16)]
    outs += both_halves(tokens, width)
    arrays = (base, *pieces, weights[5].reshape(1, -1), beside)
    scratch = [pltpu.VMEM((tokens, width), F32)]
    return feed_call(
        feed_forward_kernel, "feed_forward", layout, arrays, weights[6:9], outs, scratch
    )


def feed_both_kernel(
    info, base, whole, other, gain, incoming, gate_weight, up_weight, down_weight, *refs
):
    hidden, half, send, keep, back_send, back_keep, inner_in, total, back_total = refs

    @pl.when(pl.program_id(0) == 0)
    def _():
        feed_start(info, base, (whole, other), gain, hidden, inner_in, half)
        total[...] = jnp.zeros_like(total)
        back_total[...] = jnp.zeros_like(back_total)

    gate = product(inner_in[...], gate_weight[...])
    up = product(inner_in[...], up_weight[...])
    back_inner = product_right(incoming[...], down_weight[...])
    inner, back_gate, back_up = swiglu_back(gate, up, back_inner)
    total[...] += product(inner, down_weight[...])
    back_total[...] += product_right(back_gate, gate_weight[...])
    back_total[...] += product_right(back_up, up_weight[...])

    @pl.when(pl.program_id(0) == pl.num_programs(0) - 1)
    def _():
        part(info, total, send, keep)
        part(info, back_total, back_send, back_keep)


def feed_both(base, pieces, incoming, weights, layout):
    tokens, width = base.shape
    outs = [((tokens, width), F32), ((tokens // 2, width), BF16)]
    outs += both_halves(tokens, width) * 2
    arrays = (base, *pieces, weights[5].reshape(1, -1), incoming)
    scratch = [pltpu.VMEM((tokens, width), BF16)] + [pltpu.VMEM((tokens, width), F32)] * 2
    return feed_call(feed_both_kernel, "feed_both", layout, arrays, weights[6:9], outs, scratch)


def feed_back_kernel(
    info,
    rows,
    gain,
    back_hidden,
    whole,
    other,
    inner_in,
    gate_weight,
    up_weight,
    down_weight,
    *refs,
):
    gradient, half, back_gain, send, keep, low, total = refs

    @pl.when(pl.program_id(0) == 0)
    def _():
        def put(place, values):
            total[place, :] = values

        join(info, (whole, other), put)
        back, gains = rms_norm_back(rows[...], gain[...], total[...])
        back_gain[...] = gains
        gradient[...] = back + back_hidden[...]
        low[...] = gradient[...].astype(BF16)
        half[...] = low[halves(info, half.shape[0])[0], :]
        total[...] = jnp.zeros_like(total)

    gate = product(inner_in[...], gate_weight[...])
    up = product(inner_in[...], up_weight[...])
    back_inner = product_right(low[...], down_weight[...])
    _, back_gate, back_up = swiglu_back(gate, up, back_inner)
    total[...] += product_right(back_gate, gate_weight[...])
    total[...] += product_right(back_up, up_weight[...])

    @pl.when(pl.program_id(0) == pl.num_programs(0) - 1)
    def _():
        part(info, total, send, keep)


def feed_back(rows, gain, back_hidden, pieces, inner_in, weights, layout):
    tokens, width = rows.shape
    outs = [((tokens, width), F32), ((tokens // 2, width), BF16), ((1, width), F32)]
    outs += both_halves(tokens, width)
    arrays = (rows, gain.reshape(1, -1), back_hidden, *pieces, inner_in)
    scratch = [pltpu.VMEM((tokens, width), BF16), pltpu.VMEM((tokens, width), F32)]
    return feed_call(feed_back_kernel, "feed_back", layout, arrays, weights[6:9], outs, scratch)


def middle_back_kernel(info, hidden, incoming, whole, other, gain, projection, mixed, *refs):
    back_hidden, low, back_mixed, delta, back_gain = refs

    def put(place, values):
        back_hidden[place, :] = values

    join(info, (whole, other), put)
    back, gains = rms_norm_back(hidden[...], gain[...], back_hidden[...])
    back_gain[...] = gains
    back_hidden[...] = back + incoming[...].astype(F32)
    low[...] = back_hidden[...].astype(BF16)
    back_mixed[...] = product_right(low[...], projection[...]).astype(BF16)
    both = back_mixed[...].astype(F32) * mixed[...].astype(F32)
    for head in range(both.shape[1] // HEAD_SIZE):
        piece = both[:, head * HEAD_SIZE : (head + 1) * HEAD_SIZE].T
        delta[head : head + 1, :] = jnp.sum(piece, axis=0, keepdims=True)


def middle_back(hidden, incoming, pieces, weights, mixed, layout):
    tokens, width = hidden.shape
    wide = mixed.shape[1]
    outs = [
        ((tokens, width), F32),
        ((tokens, width), BF16),
        ((tokens, wide), BF16),
        ((wide // HEAD_SIZE, tokens), F32),
        ((1, width), F32),
    ]
    arrays = (hidden, incoming, *pieces, weights[5].reshape(1, -1), weights[4], mixed)
    return call(middle_back_kernel, "middle_back", layout.info, arrays, outs)


def pair_back_kernel(blocks, info, back_query, query_weight, key_weight, value_weight, *refs):
    cosine, sine = refs[:2]
    received = refs[2 : 2 + blocks]
    pair, send, keep, total = refs[2 + blocks :]
    width = key_weight.shape[1]
    sums = received[0][...].astype(F32)
    for term in received[1:]:
        sums += term[...].astype(F32)
    for lane in range(0, width, HEAD_SIZE):
        piece = sums[:, lane : lane + HEAD_SIZE]
        pair[:, lane : lane + HEAD_SIZE] = unrotate(piece, cosine[...], sine[...]).astype(BF16)
    pair[:, width:] = sums[:, width:].astype(BF16)
    total[...] = product_right(back_query[...], query_weight[...])
    total[...] += product_right(pair[:, :width], key_weight[...])
    total[...] += product_right(pair[:, width:], value_weight[...])
    part(info, total, send, keep)


def pair_back(received, back_query, weights, layout):
    tokens = back_query.shape[0]
    width = weights[1].shape[0]
    outs = [((tokens, received[0].shape[1]), BF16), *both_halves(tokens, width)]
    return call(
        functools.partial(pair_back_kernel, len(received)),
        "pair_back",
        layout.info,
        (back_query, *weights[1:4], *layout.tables, *received),
        outs,
        [pltpu.VMEM((tokens, width), F32)],
    )


def inputs_back_kernel(info, rows, gain, back_hidden, whole, other, gradient, back_gain):
    def put(place, values):
        gradient[place, :] = values

    join(info, (whole, other), put)
    back, gains = rms_norm_back(rows[...].astype(F32), gain[...], gradient[...])
    back_gain[...] = gains
    gradient[...] = back + back_hidden[...]


def inputs_back(rows, gain, back_hidden, pieces, layout):
    tokens, width = rows.shape
    outs = [((tokens, width), F32), ((1, width), F32)]
    arrays = (rows, gain.reshape(1, -1), back_hidden, *pieces)
    return call(inputs_back_kernel, "inputs_back", layout.info, arrays, outs)


def head_rows(ref, head, group, tokens):
    parts = []
    for member in range(group):
        lane = (head * group + member) * HEAD_SIZE
        parts.append(ref[:tokens, lane : lane + HEAD_SIZE])
    return jnp.concatenate(parts, axis=0)


def wide(row, group):
    return jnp.concatenate([row] * group, axis=1)


def seen_mask(first_row, key_start, query_start, tokens, group):
    shape = (tokens, tokens)
    key = key_start + lax.broadcasted_iota(jnp.int32, shape, 0)
    query = query_start + lax.broadcasted_iota(jnp.int32, shape, 1)
    seen = (key <= query) & (key >= first_row)
    return jnp.concatenate([seen.astype(F32)] * group, axis=1) > 0.5


def earlier_block(own, slot):
    block = slot_block(own, slot)
    return block, (block >= 0) & (block <= own)


def attend_kernel(blocks, heads, group, info, firsts, query, projection, *refs):
    pairs = refs[:blocks]
    mixed_ref, log_ref, send, keep, scores, top, total, partial = refs[blocks:]
    tokens = query.shape[0]
    own = info[0]
    first_row = firsts[pl.ds(own, 1), :]
    for head in range(heads):
        rows = head_rows(query, head, group, tokens)
        top[...] = jnp.full_like(top, NEGATIVE)
        for slot in range(blocks):
            block, valid = earlier_block(own, slot)

            @pl.when(valid)
            def _():
                keys = pairs[slot][:, head * HEAD_SIZE : (head + 1) * HEAD_SIZE]
                found = product_right(keys, rows) * SCALE
                seen = seen_mask(first_row, block * tokens, own * tokens, tokens, group)
                found = jnp.where(seen, found, NEGATIVE)
                scores[slot] = found
                top[...] = jnp.maximum(top[...], jnp.max(found, axis=0, keepdims=True))

        highest = top[0:1, :]
        total[...] = jnp.zeros_like(total)
        top[...] = jnp.zeros_like(top)
        for slot in range(blocks):
            block, valid = earlier_block(own, slot)

            @pl.when(valid)
            def _():
                lane = (heads + head) * HEAD_SIZE
                values = pairs[slot][:, lane : lane + HEAD_SIZE]
                weights = jnp.exp(scores[slot] - highest)
                top[...] += jnp.sum(weights, axis=0, keepdims=True)
                total[...] += product_left(values, weights.astype(BF16))

        mass = top[0:1, :]
        result = (total[...] / mass).T
        logs = highest + jnp.log(mass)
        for member in range(group):
            lane = (head * group + member) * HEAD_SIZE
            span = slice(member * tokens, (member + 1) * tokens)
            mixed_ref[:, lane : lane + HEAD_SIZE] = result[span].astype(BF16)
            log_ref[head * group + member : head * group + member + 1, :] = logs[:, span]


    partial[...] = product(mixed_ref[...], projection[...])
    part(info, partial, send, keep)


def attend(query, pairs, projection, layout, heads, group):
    tokens, wide = query.shape
    width = projection.shape[1]
    blocks = len(pairs)
    outs = [((tokens, wide), BF16), ((heads * group, tokens), F32), *both_halves(tokens, width)]
    scratch = [
        pltpu.VMEM((blocks, tokens, group * tokens), F32),
        pltpu.VMEM((8, group * tokens), F32),
        pltpu.VMEM((HEAD_SIZE, group * tokens), F32),
        pltpu.VMEM((tokens, width), F32),
    ]
    return call(
        functools.partial(attend_kernel, blocks, heads, group),
        "attend",
        layout.info,
        (layout.firsts, query, projection, *pairs),
        outs,
        scratch,
        limit=40,
    )


def attend_back_kernel(
    first, count, heads, group, last, info, firsts, query, back, logs, delta, cosine, sine, *refs
):
    pairs = refs[:count]
    refs = refs[count:]
    evens = count // 2
    started = len(refs) > evens + 2 + last
    if started:
        before, refs = refs[0], refs[1:]
    even, odd, out_ref = refs[:evens], refs[evens], refs[evens + 1]
    total = refs[evens + 2] if last else out_ref
    tokens = query.shape[0]
    own = info[0]
    first_row = firsts[pl.ds(own, 1), :]

    def put(index, lane, values):
        columns = slice(lane, lane + HEAD_SIZE)
        if index % 2:
            start = index // 2 * tokens
            odd[start : start + tokens, columns] = values.astype(BF16)
        else:
            even[index // 2][:, columns] = values.astype(BF16)

    for head in range(heads):
        rows = head_rows(query, head, group, tokens)
        back_rows = head_rows(back, head, group, tokens)
        members = range(head * group, (head + 1) * group)
        log_row = jnp.concatenate([logs[m : m + 1, :] for m in members], axis=1)
        delta_row = jnp.concatenate([delta[m : m + 1, :] for m in members], axis=1)
        if started:
            total[head] = before[head]
        else:
            total[head] = jnp.zeros(total.shape[1:], F32)
        lane = head * HEAD_SIZE
        value_lane = (heads + head) * HEAD_SIZE
        for index in range(count):
            block, valid = earlier_block(own, first + index)

            @pl.when(valid)
            def _():
                keys = pairs[index][:, lane : lane + HEAD_SIZE]
                values = pairs[index][:, value_lane : value_lane + HEAD_SIZE]
                found = product_right(keys, rows) * SCALE - log_row
                seen = seen_mask(first_row, block * tokens, own * tokens, tokens, group)
                probs = jnp.exp(jnp.where(seen, found, NEGATIVE))
                back_probs = product_right(values, back_rows)
                back_scores = (probs * (back_probs - delta_row) * SCALE).astype(BF16)
                total[head] += product_left(keys, back_scores)
                put(index, lane, product(back_scores, rows))
                put(index, value_lane, product(probs.astype(BF16), back_rows))

            @pl.when(jnp.logical_not(valid))
            def _():
                empty = jnp.zeros((tokens, HEAD_SIZE), F32)
                put(index, lane, empty)
                put(index, value_lane, empty)

        if last:
            result = total[head].T
            for member in range(group):
                out_lane = (head * group + member) * HEAD_SIZE
                piece = result[member * tokens : (member + 1) * tokens]
                out_ref[:, out_lane : out_lane + HEAD_SIZE] = unrotate(
                    piece, cosine[...], sine[...]
                ).astype(BF16)


def attend_back(first, query, back, logs, delta, pairs, before, last, layout, heads, group):
    tokens, width = query.shape
    count = len(pairs)
    state = (heads, HEAD_SIZE, group * tokens)
    earlier = [] if before is None else [before]
    columns = pairs[0].shape[1]
    outs = [((tokens, columns), BF16)] * (count // 2) + [((count // 2 * tokens, columns), BF16)]
    outs.append(((tokens, width), BF16) if last else (state, F32))
    return call(
        functools.partial(attend_back_kernel, first, count, heads, group, last),
        "attend_back",
        layout.info,
        (layout.firsts, query, back, logs, delta, *layout.tables, *pairs, *earlier),
        outs,
        [pltpu.VMEM(state, F32)] if last else [],
    )


def attention_back(query, back_mixed, logs, delta, pairs, layout, heads, group, beside):
    blocks = layout.blocks
    half = blocks // 2
    *even, odd, state = attend_back(
        half, query, back_mixed, logs, delta, pairs[half:], None, False, layout, heads, group
    )
    received = send_back(even, odd, half, blocks)
    *even, odd, back_query = attend_back(
        0, query, back_mixed, logs, delta, pairs[:half], state, True, layout, heads, group
    )
    received = send_back(even, odd, 0, blocks) + received
    received, done = tie(tuple(received), beside(back_query))
    return back_query, received, done


def attention_weights_kernel(blocks, info, low, mixed, normed, back_query, *refs):
    back_pair = refs[0] if len(refs) == 3 else None
    keep, send = refs[-2:]
    wide = mixed.shape[1]
    size = low.shape[1] // blocks
    parity = lax.rem(info[0], 2)
    for block in range(blocks):
        columns = slice(block * size, (block + 1) * size)
        rows = slice(block // 2 * size, (block // 2 + 1) * size)
        terms = [
            product_left(low[:, columns], mixed[...]).astype(BF16),
            product_left(normed[:, columns], back_query[...]).astype(BF16),
        ]
        if back_pair is not None:
            terms.append(product_left(normed[:, columns], back_pair[...]).astype(BF16))
        terms = jnp.concatenate(terms, axis=1)

        @pl.when(parity == block % 2)
        def _():
            keep[rows, :] = terms

        @pl.when(parity != block % 2)
        def _():
            send[rows, :] = terms


def attention_weights(low, mixed, normed, back_query, back_pair, layout):
    blocks = layout.blocks
    arrays = [low, mixed, normed, back_query] + ([] if back_pair is None else [back_pair])
    total = mixed.shape[1] + sum(array.shape[1] for array in arrays[3:])
    shape = (low.shape[1] // 2, total)
    return call(
        functools.partial(attention_weights_kernel, blocks),
        "attention_weights",
        layout.info,
        arrays,
        [(shape, BF16)] * 2,
    )


def split_kernel(share, *outs):
    start = 0
    for index, out in enumerate(outs):
        turned = index == 0
        size = out.shape[0] if turned else out.shape[1]
        piece = share[:, start : start + size].astype(F32)
        out[...] = piece.T if turned else piece
        start += size


def split_share(share, sizes):
    rows = share.shape[0]
    shapes = [(sizes[0], rows)] + [(rows, size) for size in sizes[1:]]
    return pl.pallas_call(
        split_kernel,
        out_shape=tuple(jax.ShapeDtypeStruct(shape, F32) for shape in shapes),
        in_specs=[WHOLE],
        out_specs=(WHOLE,) * len(shapes),
        compiler_params=pltpu.CompilerParams(vmem_limit_bytes=32 * 1024 * 1024),
        cost_estimate=cost("split_share"),
        name="split_share",
    )(share)


def window(place, part, width):
    return jnp.minimum(place * part // 128 * 128, width - 256)


def cut(scalars, sums, outs):
    @pl.when(pl.program_id(0) == pl.num_programs(0) - 1)
    def _():
        gate, up, down = outs
        size = gate.shape[0]
        rows = pl.ds(pl.multiple_of(scalars[1], 16), size)
        gate[...] = sums[0][rows, :]
        up[...] = sums[1][rows, :]
        down[...] = pltpu.roll(sums[2][...], 256 - scalars[1], 1)[:, :size]


def begin(started, before, outs, first):
    @pl.when(first)
    def _():
        for index, out in enumerate(outs):
            out[...] = before[index][...] if started else jnp.zeros_like(out)


def feedforward_weights_kernel(
    started, scalars, rows, incoming, gate_weight, up_weight, down_weight, *refs
):
    outs = refs[6:9] if started else refs[:3]
    begin(started, refs[:3], outs, pl.program_id(0) == 0)
    gate = product(rows[...], gate_weight[...])
    up = product(rows[...], up_weight[...])
    back_inner = product_right(incoming[...], down_weight[...])
    inner, back_gate, back_up = swiglu_back(gate, up, back_inner)
    columns = pl.ds(pl.multiple_of(scalars[0], 128), 256)
    rows_part, incoming_part = rows[:, columns], incoming[:, columns]
    outs[0][...] += product_left(rows_part, back_gate)
    outs[1][...] += product_left(rows_part, back_up)
    outs[2][...] += product_left(inner, incoming_part)
    if started:
        cut(scalars, outs, refs[3:6])


def feedforward_prepare_kernel(rows, gate_weight, up_weight, inner_out, gate_out, up_out):
    gate = product(rows[...], gate_weight[...])
    up = product(rows[...], up_weight[...])
    chance = 1.0 / (1.0 + jnp.exp(-gate))
    silu = gate * chance
    inner_out[...] = (silu * up).astype(BF16)
    gate_out[...] = (up * (chance + silu * (1.0 - chance))).astype(BF16)
    up_out[...] = silu.astype(BF16)


def feedforward_finish_kernel(
    started, scalars, rows, incoming, inner, gate_slope, up_slope, down_weight, *refs
):
    outs = refs[6:9] if started else refs[:3]
    begin(started, refs[:3], outs, pl.program_id(0) == 0)
    back_inner = product_right(incoming[...], down_weight[...])
    back_gate = (back_inner * gate_slope[...].astype(F32)).astype(BF16)
    back_up = (back_inner * up_slope[...].astype(F32)).astype(BF16)
    columns = pl.ds(pl.multiple_of(scalars[0], 128), 256)
    rows_part, incoming_part = rows[:, columns], incoming[:, columns]
    outs[0][...] += product_left(rows_part, back_gate)
    outs[1][...] += product_left(rows_part, back_up)
    outs[2][...] += product_left(inner[...], incoming_part)
    if started:
        cut(scalars, outs, refs[3:6])


STEP = 256


def fixed(shape):
    return pl.BlockSpec(shape, lambda i: (0,) * len(shape), pipeline_mode=pl.Buffered(1))


def moving(columns, offset=0):
    return pl.BlockSpec((STEP, columns), lambda i: (i + offset, 0))


def weight_call(kernel, name, layout, moved, still, hidden, steps, before):
    width = moved[0][1][-1]
    shapes = [(256, hidden), (256, hidden), (hidden, 256)]
    started = before is not None
    earlier = list(before) if started else []
    kept = lambda shape: pl.BlockSpec(
        shape, lambda i, s: (0,) * len(shape), pipeline_mode=pl.Buffered(1)
    )
    size = width // layout.blocks
    own = window(layout.own, size, width)
    place = jnp.stack([own, layout.own * size - own])
    outs = [(size, hidden), (size, hidden), (hidden, size)] if started else shapes
    return pl.pallas_call(
        functools.partial(kernel, started),
        out_shape=tuple(jax.ShapeDtypeStruct(shape, F32) for shape in outs),
        grid_spec=pltpu.PrefetchScalarGridSpec(
            num_scalar_prefetch=1,
            grid=(steps,),
            in_specs=[pl.BlockSpec(block, place) for _, block, place in moved]
            + [kept(array.shape) for array in still]
            + ([kept(shape) for shape in shapes] if started else []),
            out_specs=tuple(kept(shape) for shape in outs),
            scratch_shapes=[pltpu.VMEM(shape, F32) for shape in shapes] if started else [],
        ),
        compiler_params=pltpu.CompilerParams(vmem_limit_bytes=48 * MEGA),
        cost_estimate=cost(name),
        name=name,
    )(place, *[array for array, _, _ in moved], *still, *earlier)


def feedforward_weights(rows, incoming, weights, layout, before):
    total, width = rows.shape
    steps = total // STEP
    moved = [
        (rows, (STEP, width), lambda i, s: (i, 0)),
        (incoming, (STEP, width), lambda i, s: (i, 1)),
    ]
    return weight_call(
        feedforward_weights_kernel,
        "feedforward_weights",
        layout,
        moved,
        weights[6:9],
        weights[6].shape[1],
        steps,
        before,
    )


def feedforward_finish(rows, incoming, prepared, weights, layout, before):
    width = weights[6].shape[0]
    moved = [
        (array, (STEP, min(width, array.shape[1])), lambda i, s: (i, 0))
        for array in (rows, incoming, *prepared)
    ]
    return weight_call(
        feedforward_finish_kernel,
        "feedforward_finish",
        layout,
        moved,
        weights[8:9],
        weights[6].shape[1],
        rows.shape[0] // STEP,
        before,
    )


def feedforward_prepare(rows, weights):
    total, width = rows.shape[0], weights[6].shape[0]
    hidden = weights[6].shape[1]
    return pl.pallas_call(
        feedforward_prepare_kernel,
        grid=(total // STEP,),
        out_shape=(jax.ShapeDtypeStruct((total, hidden), BF16),) * 3,
        in_specs=[moving(width), fixed((width, hidden)), fixed((width, hidden))],
        out_specs=(moving(hidden),) * 3,
        compiler_params=pltpu.CompilerParams(vmem_limit_bytes=48 * 1024 * 1024),
        cost_estimate=cost("feedforward_prepare"),
        name="feedforward_prepare",
    )(rows, weights[6], weights[7])


def swiglu_back(gate, up, back_inner):
    chance = 1.0 / (1.0 + jnp.exp(-gate))
    silu = gate * chance
    inner = (silu * up).astype(BF16)
    back_gate = (back_inner * up * (chance + silu * (1.0 - chance))).astype(BF16)
    back_up = (back_inner * silu).astype(BF16)
    return inner, back_gate, back_up


class Layout:
    def __init__(self, lengths, tokens):
        self.tokens = tokens
        self.blocks = lax.axis_size("blk")
        self.own = lax.axis_index("blk")
        self.core = lax.rem(lax.axis_index("tp"), 2)
        index = jnp.arange(tokens * self.blocks, dtype=jnp.int32)
        firsts = first_tokens(lengths, index)
        mine = lax.dynamic_slice_in_dim(index - firsts, self.own * tokens, tokens, 0)
        self.tables = rotary_tables(mine)
        self.firsts = firsts.reshape(self.blocks, tokens)
        self.info = jnp.stack([self.own, self.core]).astype(jnp.int32)


def attention_share(normed, back_rows, blocks):
    return sum_blocks(product_left(normed, back_rows).astype(BF16), blocks)


def body(tokens, lengths, *rest):
    one, two, cotangent = rest[:9], rest[9:18], rest[18]
    layout = Layout(lengths, tokens.shape[0])
    core, blocks = layout.core, layout.blocks
    heads = one[2].shape[1] // HEAD_SIZE
    group = one[1].shape[1] // HEAD_SIZE // heads

    wide, narrow = one[1].shape[1], one[2].shape[1]

    normed_one, query_one, pair_one = front(tokens, None, one, layout)
    pairs_one = gather_pairs(pair_one, blocks)
    mixed_one, logs_one, send, keep = attend(query_one, pairs_one, one[4], layout, heads, group)
    hidden_one, inner_in_one, half_one, send, keep = feed_forward(
        tokens, sum_tp(send, keep), cotangent, one, layout
    )
    pieces = sum_tp(send, keep)
    rows_one = gather_rows(half_one)

    normed_two, query_two, pair_two, inputs_two = front(hidden_one, pieces, two, layout)
    pairs_two = gather_pairs(pair_two, blocks)
    mixed_two, logs_two, send, keep = attend(query_two, pairs_two, two[4], layout, heads, group)

    def prepare(rows, after):
        return feedforward_prepare(tie(after, rows)[1], one)

    pieces = sum_tp(send, keep)

    hidden_two, half_two, last_send, last_keep, send, keep = feed_both(
        inputs_two, pieces, cotangent, two, layout
    )
    rows_two = gather_rows(half_two)

    pieces = sum_tp(send, keep)
    back_hidden, low, back_mixed, delta, gain_feed_two = middle_back(
        hidden_two, cotangent, pieces, two, mixed_two, layout
    )

    def finish_forward(after):
        whole, other = sum_tp(tie(after, last_send)[1], last_keep)
        top, bottom = jnp.where(core == 0, whole, other), jnp.where(core == 0, other, whole)
        last = jnp.concatenate([top, bottom], axis=0).astype(F32)
        prepared_own = prepare(rows_one[0], after)
        prepared_other = prepare(rows_one[1], prepared_own[0])
        return (hidden_two + last).astype(BF16), prepared_own, prepared_other

    back_query, received, (result, prepared_own, prepared_other) = attention_back(
        query_two, back_mixed, logs_two, delta, pairs_two, layout, heads, group, finish_forward
    )
    back_pair, send, keep = pair_back(received, back_query, two, layout)

    state = [None]
    early = [None]

    def weights_two(piece):
        rows, incoming = early[0][piece], rows_one[piece]

        def run(after):
            held, rows_now, incoming_now = tie(after, rows, incoming)
            state[0] = feedforward_weights(
                rows_now, incoming_now, two, layout, state[0]
            )
            return state[0]

        return run

    terms_two = (low, mixed_two, normed_two, back_query, back_pair)

    def share_second(after):
        terms = tie(after, *terms_two)[1:]
        return attention_weights(*terms, layout)

    pieces, bucket_two = sum_tp(send, keep, share_second)

    gradient, half_low, gain_attention_two, send, keep = feed_back(
        inputs_two, two[0], back_hidden, pieces, inner_in_one, one, layout
    )

    pieces = sum_tp(send, keep)
    half_low, pieces = tie(half_low, pieces)
    early[0] = rows_two
    ends = gather_rows(half_low)
    share_two = scatter_blocks(sum_pair(*bucket_two, blocks), blocks)
    back_hidden, low, back_mixed, delta, gain_feed_one = middle_back(
        hidden_one, gradient, pieces, one, mixed_one, layout
    )
    back_query, received, state[0] = attention_back(
        query_one, back_mixed, logs_one, delta, pairs_one, layout, heads, group, weights_two(0)
    )
    back_pair, send, keep = pair_back(received, back_query, one, layout)

    def share_first(after):
        terms = tie(after, low, mixed_one, normed_one, back_query)[1:]
        return attention_weights(*terms, None, layout), weights_two(1)(after)

    pieces, (bucket_one, state[0]) = sum_tp(send, keep, share_first)
    share_one = scatter_blocks(sum_pair(*bucket_one, blocks), blocks)
    tokens_gradient, gain_attention_one = inputs_back(tokens, one[0], back_hidden, pieces, layout)
    feed_two = state[0]
    feed_one = None
    for rows, end, prepared in zip(rows_one, ends, (prepared_own, prepared_other)):
        feed_one = feedforward_finish(rows, end, prepared, one, layout, feed_one)
    share_pair_one = attention_share(normed_one, back_pair, blocks)
    projection_two, *others_two = split_share(share_two, (wide, wide, narrow, narrow))
    projection_one, gradient_query_one = split_share(share_one, (wide, wide))
    shares_two = (*others_two, projection_two)
    shares_one = (
        gradient_query_one,
        share_pair_one[:, :narrow],
        share_pair_one[:, narrow:],
        projection_one,
    )
    gains = jnp.stack([gain_attention_one, gain_feed_one, gain_attention_two, gain_feed_two])
    gains, feed_one = tie(gains, tuple(feed_one))
    gains = gains.reshape(4, blocks, -1).transpose(1, 0, 2)
    gains = jnp.sum(lax.all_to_all(gains, "blk", 0, 0, tiled=True), axis=0)
    return (
        (result, tokens_gradient)
        + (gains[0],)
        + shares_one
        + (gains[1],)
        + tuple(feed_one)
        + (gains[2],)
        + shares_two
        + (gains[3],)
        + tuple(feed_two)
    )


def solution(mesh):
    rows, columns = P("tp", None), P(None, "tp")
    layer = (P(), columns, columns, columns, rows, P(), columns, columns, rows)
    in_specs = (P("blk", None), P()) + layer + layer + (P("blk", None),)
    wide_out, tall_out = P("blk", "tp"), P("tp", "blk")
    layer_out = (
        P("blk"),
        wide_out,
        wide_out,
        wide_out,
        tall_out,
        P("blk"),
        wide_out,
        wide_out,
        tall_out,
    )
    out_specs = (P("blk", None), P("blk", None)) + layer_out + layer_out
    return jax.shard_map(body, mesh=mesh, in_specs=in_specs, out_specs=out_specs, check_vma=False)
```

```python
import functools

import jax
import jax.numpy as jnp
from jax import lax
from jax.experimental import pallas as pl
from jax.experimental.pallas import tpu as pltpu
from jax.sharding import PartitionSpec as P

HEAD_SIZE = 96
EPSILON = 1e-05
ROTARY_BASE = 100000.0
NEGATIVE = -1e30
SCALE = HEAD_SIZE ** (-0.5)
BF16 = jnp.bfloat16
F32 = jnp.float32


def product(left, right):
    return jnp.dot(left, right, preferred_element_type=F32)


def product_left(left, right):
    return lax.dot_general(left, right, (((0,), (0,)), ((), ())), preferred_element_type=F32)


def product_right(left, right):
    return lax.dot_general(left, right, (((1,), (1,)), ((), ())), preferred_element_type=F32)


def rms_norm(rows, gain):
    return rows * lax.rsqrt(jnp.mean(rows * rows, axis=-1, keepdims=True) + EPSILON) * gain


def rms_norm_back(rows, gain, incoming):
    scale = lax.rsqrt(jnp.mean(rows * rows, axis=-1, keepdims=True) + EPSILON)
    weighted = incoming * gain
    inner = jnp.mean(rows * weighted, axis=-1, keepdims=True)
    back = scale * weighted - rows * (scale * scale * scale * inner)
    return back, jnp.sum(incoming * rows * scale, axis=0, keepdims=True)


def rotate(rows, cosine, sine):
    half = HEAD_SIZE // 2
    turned = jnp.concatenate([-rows[..., half:], rows[..., :half]], axis=-1)
    return rows * cosine + turned * sine


def unrotate(rows, cosine, sine):
    half = HEAD_SIZE // 2
    scaled = rows * sine
    return rows * cosine + jnp.concatenate([scaled[..., half:], -scaled[..., :half]], axis=-1)


def rotary_tables(positions):
    half = HEAD_SIZE // 2
    rates = ROTARY_BASE ** (-(jnp.arange(half).astype(F32) * 2.0 / HEAD_SIZE))
    angle = positions.astype(F32)[:, None] * rates[None, :]
    angle = jnp.concatenate([angle, angle], axis=-1)
    return jnp.cos(angle), jnp.sin(angle)


def first_tokens(lengths, index):
    bounds = jnp.cumsum(lengths)
    starts = bounds - lengths
    owner = jnp.sum((index[:, None] >= bounds[None, :]).astype(jnp.int32), axis=1)
    picks = owner[:, None] == jnp.arange(lengths.shape[0], dtype=jnp.int32)[None, :]
    return jnp.sum(jnp.where(picks, starts[None, :], 0), axis=1).astype(jnp.int32)


def swap(rows, axis, size, bit):
    return lax.ppermute(rows, axis, [(i, i ^ bit) for i in range(size)])


def tie(*values):
    return lax.optimization_barrier(values)


def sum_tp(send, keep, beside=None):
    pair = (keep + swap(send, "tp", 4, 1).astype(F32)).astype(BF16)
    moved = swap(pair, "tp", 4, 2)
    done = None
    if beside is not None:
        moved, done = tie(moved, beside(pair))
    whole = (pair.astype(F32) + moved.astype(F32)).astype(BF16)
    pieces = whole, swap(whole, "tp", 4, 1)
    return pieces if beside is None else (pieces, done)


def slot_block(own, slot):
    return (own // 2 - slot // 2) * 2 + own % 2 + slot % 2 * (1 - 2 * (own % 2))


def gather_pairs(rows, blocks):
    slots = []
    for far in range(blocks // 2):
        pairs = [(i, i + 2 * far) for i in range(blocks - 2 * far)]
        slots.append(lax.ppermute(rows, "blk", pairs) if far else rows)
    return [part for near in slots for part in (near, swap(near, "blk", blocks, 1))]


def send_back(even, odd, first, blocks):
    other = swap(odd, "blk", blocks, 1)
    rows = even[0].shape[0]
    received = []
    for index, term in enumerate(even):
        theirs = other[index * rows : (index + 1) * rows]
        both = (term.astype(F32) + theirs.astype(F32)).astype(BF16)
        far = first // 2 + index
        pairs = [(i, i - 2 * far) for i in range(2 * far, blocks)]
        received.append(lax.ppermute(both, "blk", pairs) if far else both)
    return received


def sum_blocks(partial, blocks):
    rows, columns = partial.shape
    parts = lax.all_to_all(partial, "blk", 0, 0, tiled=True).reshape(blocks, -1, columns)
    return jnp.sum(parts.astype(F32), axis=0)


def sum_pair(keep, send, blocks):
    return (keep.astype(F32) + swap(send, "blk", blocks, 1).astype(F32)).astype(BF16)


def scatter_blocks(both, blocks):
    groups = [list(range(parity, blocks, 2)) for parity in range(2)]
    return lax.psum_scatter(
        both, "blk", scatter_dimension=0, axis_index_groups=groups, tiled=True
    )


def gather_rows(half):
    own = lax.all_gather(half, "blk", axis=0, tiled=True)
    return own, swap(own, "tp", 4, 1)


WHOLE = pl.BlockSpec(memory_space=pltpu.VMEM)
SCALARS = pl.BlockSpec(memory_space=pltpu.SMEM)
MEGA = 1024 * 1024
TIMES = dict(
    front=2.5,
    attend=8,
    feed_forward=7,
    feed_both=9,
    feed_back=12,
    middle_back=2.5,
    attend_back=6,
    pair_back=2,
    inputs_back=3,
    feedforward_prepare=11,
    feedforward_weights=17.5,
    feedforward_finish=10.5,
    attention_weights=2.5,
    split_share=1,
)


def cost(name):
    return pl.CostEstimate(
        flops=int(TIMES[name] * TIME_FLOPS), bytes_accessed=0, transcendentals=0
    )


TIME_FLOPS = 1.3e9


def shaped(*shapes):
    return tuple(jax.ShapeDtypeStruct(shape, kind) for shape, kind in shapes)


def call(kernel, name, info, arrays, outs, scratch=(), limit=32, **more):
    more.setdefault("in_specs", [SCALARS] + [WHOLE] * len(arrays))
    more.setdefault("out_specs", (WHOLE,) * len(outs))
    return pl.pallas_call(
        kernel,
        out_shape=shaped(*outs),
        scratch_shapes=list(scratch),
        compiler_params=pltpu.CompilerParams(vmem_limit_bytes=limit * MEGA),
        cost_estimate=cost(name),
        name=name,
        **more,
    )(info, *arrays)


def halves(info, half):
    start = pl.multiple_of(info[1] * half, half)
    return pl.ds(start, half), pl.ds(pl.multiple_of(half - start, half), half)


def join(info, pieces, put):
    whole, other = pieces
    mine, theirs = halves(info, whole.shape[0])
    put(mine, whole[...].astype(F32))
    put(theirs, other[...].astype(F32))


def part(info, total, send, keep):
    mine, theirs = halves(info, keep.shape[0])
    keep[...] = total[mine, :]
    send[...] = total[theirs, :].astype(BF16)


def both_halves(tokens, width):
    return ((tokens // 2, width), BF16), ((tokens // 2, width), F32)


def front_kernel(joined, info, base, *refs):
    if joined:
        whole, other = refs[:2]
        refs = refs[2:]
    gain, query_weight, key_weight, value_weight, cosine, sine = refs[:6]
    normed, query, pair = refs[6:9]
    if joined:
        inputs = refs[9]

        def put(rows, values):
            inputs[rows, :] = base[rows, :] + values

        join(info, (whole, other), put)
        source = inputs[...]
    else:
        source = base[...].astype(F32)
    normed[...] = rms_norm(source, gain[...]).astype(BF16)

    def turned(weight, out):
        rows = product(normed[...], weight[...])
        for lane in range(0, weight.shape[1], HEAD_SIZE):
            piece = rows[:, lane : lane + HEAD_SIZE]
            out[:, lane : lane + HEAD_SIZE] = rotate(piece, cosine[...], sine[...]).astype(BF16)

    turned(key_weight, pair)
    pair[:, key_weight.shape[1] :] = product(normed[...], value_weight[...]).astype(BF16)
    turned(query_weight, query)


def front(base, pieces, weights, layout):
    tokens, width = base.shape
    wide, narrow = weights[1].shape[1], weights[2].shape[1]
    joined = pieces is not None
    arrays = (base,) + (pieces if joined else ()) + (weights[0].reshape(1, -1),)
    arrays += tuple(weights[1:4]) + layout.tables
    outs = [((tokens, width), BF16), ((tokens, wide), BF16), ((tokens, 2 * narrow), BF16)]
    if joined:
        outs.append(((tokens, width), F32))
    return call(functools.partial(front_kernel, joined), "front", layout.info, arrays, outs)


def feed_specs(arrays, weights, chunk):
    width = weights[0].shape[0]
    across = pl.BlockSpec((width, chunk), lambda i: (0, i))
    down = pl.BlockSpec((chunk, width), lambda i: (i, 0))
    return [SCALARS] + [fixed(array.shape) for array in arrays] + [across, across, down]


def feed_call(kernel, name, layout, arrays, weights, outs, scratch):
    chunk = 256
    return call(
        kernel,
        name,
        layout.info,
        tuple(arrays) + tuple(weights),
        outs,
        scratch,
        limit=40,
        grid=(weights[0].shape[1] // chunk,),
        in_specs=feed_specs(arrays, weights, chunk),
        out_specs=tuple(fixed(shape) for shape, _ in outs),
    )


def feed_start(info, base, pieces, gain, hidden, inner_in, half):
    def put(rows, values):
        hidden[rows, :] = base[rows, :].astype(F32) + values

    join(info, pieces, put)
    inner_in[...] = rms_norm(hidden[...], gain[...]).astype(BF16)
    half[...] = inner_in[halves(info, half.shape[0])[0], :]


def feed_forward_kernel(
    info, base, whole, other, gain, beside, gate_weight, up_weight, down_weight, *refs
):
    hidden, inner_in, half, send, keep, total = refs

    @pl.when(pl.program_id(0) == 0)
    def _():
        width = base.shape[1]
        feed_start(info, base, (whole, other), gain, hidden, inner_in, half.at[:, :width])
        half[:, width:] = beside[halves(info, half.shape[0])[0], :]
        total[...] = jnp.zeros_like(total)

    gate = product(inner_in[...], gate_weight[...])
    up = product(inner_in[...], up_weight[...])
    inner = (gate / (1.0 + jnp.exp(-gate)) * up).astype(BF16)
    total[...] += product(inner, down_weight[...])

    @pl.when(pl.program_id(0) == pl.num_programs(0) - 1)
    def _():
        part(info, total, send, keep)


def feed_forward(base, pieces, beside, weights, layout):
    tokens, width = base.shape
    outs = [((tokens, width), F32), ((tokens, width), BF16), ((tokens // 2, 2 * width), BF16)]
    outs += both_halves(tokens, width)
    arrays = (base, *pieces, weights[5].reshape(1, -1), beside)
    scratch = [pltpu.VMEM((tokens, width), F32)]
    return feed_call(
        feed_forward_kernel, "feed_forward", layout, arrays, weights[6:9], outs, scratch
    )


def feed_both_kernel(
    info, base, whole, other, gain, incoming, gate_weight, up_weight, down_weight, *refs
):
    hidden, half, send, keep, back_send, back_keep, inner_in, total, back_total = refs

    @pl.when(pl.program_id(0) == 0)
    def _():
        feed_start(info, base, (whole, other), gain, hidden, inner_in, half)
        total[...] = jnp.zeros_like(total)
        back_total[...] = jnp.zeros_like(back_total)

    gate = product(inner_in[...], gate_weight[...])
    up = product(inner_in[...], up_weight[...])
    back_inner = product_right(incoming[...], down_weight[...])
    inner, back_gate, back_up = swiglu_back(gate, up, back_inner)
    total[...] += product(inner, down_weight[...])
    back_total[...] += product_right(back_gate, gate_weight[...])
    back_total[...] += product_right(back_up, up_weight[...])

    @pl.when(pl.program_id(0) == pl.num_programs(0) - 1)
    def _():
        part(info, total, send, keep)
        part(info, back_total, back_send, back_keep)


def feed_both(base, pieces, incoming, weights, layout):
    tokens, width = base.shape
    outs = [((tokens, width), F32), ((tokens // 2, width), BF16)]
    outs += both_halves(tokens, width) * 2
    arrays = (base, *pieces, weights[5].reshape(1, -1), incoming)
    scratch = [pltpu.VMEM((tokens, width), BF16)] + [pltpu.VMEM((tokens, width), F32)] * 2
    return feed_call(feed_both_kernel, "feed_both", layout, arrays, weights[6:9], outs, scratch)


def feed_back_kernel(
    info,
    rows,
    gain,
    back_hidden,
    whole,
    other,
    inner_in,
    gate_weight,
    up_weight,
    down_weight,
    *refs,
):
    gradient, half, back_gain, send, keep, low, total = refs

    @pl.when(pl.program_id(0) == 0)
    def _():
        def put(place, values):
            total[place, :] = values

        join(info, (whole, other), put)
        back, gains = rms_norm_back(rows[...], gain[...], total[...])
        back_gain[...] = gains
        gradient[...] = back + back_hidden[...]
        low[...] = gradient[...].astype(BF16)
        half[...] = low[halves(info, half.shape[0])[0], :]
        total[...] = jnp.zeros_like(total)

    gate = product(inner_in[...], gate_weight[...])
    up = product(inner_in[...], up_weight[...])
    back_inner = product_right(low[...], down_weight[...])
    _, back_gate, back_up = swiglu_back(gate, up, back_inner)
    total[...] += product_right(back_gate, gate_weight[...])
    total[...] += product_right(back_up, up_weight[...])

    @pl.when(pl.program_id(0) == pl.num_programs(0) - 1)
    def _():
        part(info, total, send, keep)


def feed_back(rows, gain, back_hidden, pieces, inner_in, weights, layout):
    tokens, width = rows.shape
    outs = [((tokens, width), F32), ((tokens // 2, width), BF16), ((1, width), F32)]
    outs += both_halves(tokens, width)
    arrays = (rows, gain.reshape(1, -1), back_hidden, *pieces, inner_in)
    scratch = [pltpu.VMEM((tokens, width), BF16), pltpu.VMEM((tokens, width), F32)]
    return feed_call(feed_back_kernel, "feed_back", layout, arrays, weights[6:9], outs, scratch)


def middle_back_kernel(info, hidden, incoming, whole, other, gain, projection, mixed, *refs):
    back_hidden, low, back_mixed, delta, back_gain = refs

    def put(place, values):
        back_hidden[place, :] = values

    join(info, (whole, other), put)
    back, gains = rms_norm_back(hidden[...], gain[...], back_hidden[...])
    back_gain[...] = gains
    back_hidden[...] = back + incoming[...].astype(F32)
    low[...] = back_hidden[...].astype(BF16)
    back_mixed[...] = product_right(low[...], projection[...]).astype(BF16)
    both = back_mixed[...].astype(F32) * mixed[...].astype(F32)
    for head in range(both.shape[1] // HEAD_SIZE):
        piece = both[:, head * HEAD_SIZE : (head + 1) * HEAD_SIZE].T
        delta[head : head + 1, :] = jnp.sum(piece, axis=0, keepdims=True)


def middle_back(hidden, incoming, pieces, weights, mixed, layout):
    tokens, width = hidden.shape
    wide = mixed.shape[1]
    outs = [
        ((tokens, width), F32),
        ((tokens, width), BF16),
        ((tokens, wide), BF16),
        ((wide // HEAD_SIZE, tokens), F32),
        ((1, width), F32),
    ]
    arrays = (hidden, incoming, *pieces, weights[5].reshape(1, -1), weights[4], mixed)
    return call(middle_back_kernel, "middle_back", layout.info, arrays, outs)


def pair_back_kernel(blocks, info, back_query, query_weight, key_weight, value_weight, *refs):
    cosine, sine = refs[:2]
    received = refs[2 : 2 + blocks]
    pair, send, keep, total = refs[2 + blocks :]
    width = key_weight.shape[1]
    sums = received[0][...].astype(F32)
    for term in received[1:]:
        sums += term[...].astype(F32)
    for lane in range(0, width, HEAD_SIZE):
        piece = sums[:, lane : lane + HEAD_SIZE]
        pair[:, lane : lane + HEAD_SIZE] = unrotate(piece, cosine[...], sine[...]).astype(BF16)
    pair[:, width:] = sums[:, width:].astype(BF16)
    total[...] = product_right(back_query[...], query_weight[...])
    total[...] += product_right(pair[:, :width], key_weight[...])
    total[...] += product_right(pair[:, width:], value_weight[...])
    part(info, total, send, keep)


def pair_back(received, back_query, weights, layout):
    tokens = back_query.shape[0]
    width = weights[1].shape[0]
    outs = [((tokens, received[0].shape[1]), BF16), *both_halves(tokens, width)]
    return call(
        functools.partial(pair_back_kernel, len(received)),
        "pair_back",
        layout.info,
        (back_query, *weights[1:4], *layout.tables, *received),
        outs,
        [pltpu.VMEM((tokens, width), F32)],
    )


def inputs_back_kernel(info, rows, gain, back_hidden, whole, other, gradient, back_gain):
    def put(place, values):
        gradient[place, :] = values

    join(info, (whole, other), put)
    back, gains = rms_norm_back(rows[...].astype(F32), gain[...], gradient[...])
    back_gain[...] = gains
    gradient[...] = back + back_hidden[...]


def inputs_back(rows, gain, back_hidden, pieces, layout):
    tokens, width = rows.shape
    outs = [((tokens, width), F32), ((1, width), F32)]
    arrays = (rows, gain.reshape(1, -1), back_hidden, *pieces)
    return call(inputs_back_kernel, "inputs_back", layout.info, arrays, outs)


def head_rows(ref, head, group, tokens):
    parts = []
    for member in range(group):
        lane = (head * group + member) * HEAD_SIZE
        parts.append(ref[:tokens, lane : lane + HEAD_SIZE])
    return jnp.concatenate(parts, axis=0)


def wide(row, group):
    return jnp.concatenate([row] * group, axis=1)


def seen_mask(first_row, key_start, query_start, tokens, group):
    shape = (tokens, tokens)
    key = key_start + lax.broadcasted_iota(jnp.int32, shape, 0)
    query = query_start + lax.broadcasted_iota(jnp.int32, shape, 1)
    seen = (key <= query) & (key >= first_row)
    return jnp.concatenate([seen.astype(F32)] * group, axis=1) > 0.5


def earlier_block(own, slot):
    block = slot_block(own, slot)
    return block, (block >= 0) & (block <= own)


def attend_kernel(blocks, heads, group, info, firsts, query, projection, *refs):
    pairs = refs[:blocks]
    mixed_ref, log_ref, send, keep, scores, top, total, partial = refs[blocks:]
    tokens = query.shape[0]
    own = info[0]
    first_row = firsts[pl.ds(own, 1), :]
    for head in range(heads):
        rows = head_rows(query, head, group, tokens)
        top[...] = jnp.full_like(top, NEGATIVE)
        for slot in range(blocks):
            block, valid = earlier_block(own, slot)

            @pl.when(valid)
            def _():
                keys = pairs[slot][:, head * HEAD_SIZE : (head + 1) * HEAD_SIZE]
                found = product_right(keys, rows) * SCALE
                seen = seen_mask(first_row, block * tokens, own * tokens, tokens, group)
                found = jnp.where(seen, found, NEGATIVE)
                scores[slot] = found
                top[...] = jnp.maximum(top[...], jnp.max(found, axis=0, keepdims=True))

        highest = top[0:1, :]
        total[...] = jnp.zeros_like(total)
        top[...] = jnp.zeros_like(top)
        for slot in range(blocks):
            block, valid = earlier_block(own, slot)

            @pl.when(valid)
            def _():
                lane = (heads + head) * HEAD_SIZE
                values = pairs[slot][:, lane : lane + HEAD_SIZE]
                weights = jnp.exp(scores[slot] - highest)
                top[...] += jnp.sum(weights, axis=0, keepdims=True)
                total[...] += product_left(values, weights.astype(BF16))

        mass = top[0:1, :]
        result = (total[...] / mass).T
        logs = highest + jnp.log(mass)
        for member in range(group):
            lane = (head * group + member) * HEAD_SIZE
            span = slice(member * tokens, (member + 1) * tokens)
            mixed_ref[:, lane : lane + HEAD_SIZE] = result[span].astype(BF16)
            log_ref[head * group + member : head * group + member + 1, :] = logs[:, span]


    partial[...] = product(mixed_ref[...], projection[...])
    part(info, partial, send, keep)


def attend(query, pairs, projection, layout, heads, group):
    tokens, wide = query.shape
    width = projection.shape[1]
    blocks = len(pairs)
    outs = [((tokens, wide), BF16), ((heads * group, tokens), F32), *both_halves(tokens, width)]
    scratch = [
        pltpu.VMEM((blocks, tokens, group * tokens), F32),
        pltpu.VMEM((8, group * tokens), F32),
        pltpu.VMEM((HEAD_SIZE, group * tokens), F32),
        pltpu.VMEM((tokens, width), F32),
    ]
    return call(
        functools.partial(attend_kernel, blocks, heads, group),
        "attend",
        layout.info,
        (layout.firsts, query, projection, *pairs),
        outs,
        scratch,
        limit=40,
    )


def attend_back_kernel(
    first, count, heads, group, last, info, firsts, query, back, logs, delta, cosine, sine, *refs
):
    pairs = refs[:count]
    refs = refs[count:]
    evens = count // 2
    started = len(refs) > evens + 2 + last
    if started:
        before, refs = refs[0], refs[1:]
    even, odd, out_ref = refs[:evens], refs[evens], refs[evens + 1]
    total = refs[evens + 2] if last else out_ref
    tokens = query.shape[0]
    own = info[0]
    first_row = firsts[pl.ds(own, 1), :]

    def put(index, lane, values):
        columns = slice(lane, lane + HEAD_SIZE)
        if index % 2:
            start = index // 2 * tokens
            odd[start : start + tokens, columns] = values.astype(BF16)
        else:
            even[index // 2][:, columns] = values.astype(BF16)

    for head in range(heads):
        rows = head_rows(query, head, group, tokens)
        back_rows = head_rows(back, head, group, tokens)
        members = range(head * group, (head + 1) * group)
        log_row = jnp.concatenate([logs[m : m + 1, :] for m in members], axis=1)
        delta_row = jnp.concatenate([delta[m : m + 1, :] for m in members], axis=1)
        if started:
            total[head] = before[head]
        else:
            total[head] = jnp.zeros(total.shape[1:], F32)
        lane = head * HEAD_SIZE
        value_lane = (heads + head) * HEAD_SIZE
        for index in range(count):
            block, valid = earlier_block(own, first + index)

            @pl.when(valid)
            def _():
                keys = pairs[index][:, lane : lane + HEAD_SIZE]
                values = pairs[index][:, value_lane : value_lane + HEAD_SIZE]
                found = product_right(keys, rows) * SCALE - log_row
                seen = seen_mask(first_row, block * tokens, own * tokens, tokens, group)
                probs = jnp.exp(jnp.where(seen, found, NEGATIVE))
                back_probs = product_right(values, back_rows)
                back_scores = (probs * (back_probs - delta_row) * SCALE).astype(BF16)
                total[head] += product_left(keys, back_scores)
                put(index, lane, product(back_scores, rows))
                put(index, value_lane, product(probs.astype(BF16), back_rows))

            @pl.when(jnp.logical_not(valid))
            def _():
                empty = jnp.zeros((tokens, HEAD_SIZE), F32)
                put(index, lane, empty)
                put(index, value_lane, empty)

        if last:
            result = total[head].T
            for member in range(group):
                out_lane = (head * group + member) * HEAD_SIZE
                piece = result[member * tokens : (member + 1) * tokens]
                out_ref[:, out_lane : out_lane + HEAD_SIZE] = unrotate(
                    piece, cosine[...], sine[...]
                ).astype(BF16)


def attend_back(first, query, back, logs, delta, pairs, before, last, layout, heads, group):
    tokens, width = query.shape
    count = len(pairs)
    state = (heads, HEAD_SIZE, group * tokens)
    earlier = [] if before is None else [before]
    columns = pairs[0].shape[1]
    outs = [((tokens, columns), BF16)] * (count // 2) + [((count // 2 * tokens, columns), BF16)]
    outs.append(((tokens, width), BF16) if last else (state, F32))
    return call(
        functools.partial(attend_back_kernel, first, count, heads, group, last),
        "attend_back",
        layout.info,
        (layout.firsts, query, back, logs, delta, *layout.tables, *pairs, *earlier),
        outs,
        [pltpu.VMEM(state, F32)] if last else [],
    )


def attention_back(query, back_mixed, logs, delta, pairs, layout, heads, group, beside):
    blocks = layout.blocks
    half = blocks // 2
    *even, odd, state = attend_back(
        half, query, back_mixed, logs, delta, pairs[half:], None, False, layout, heads, group
    )
    received = send_back(even, odd, half, blocks)
    *even, odd, back_query = attend_back(
        0, query, back_mixed, logs, delta, pairs[:half], state, True, layout, heads, group
    )
    received = send_back(even, odd, 0, blocks) + received
    received, done = tie(tuple(received), beside(back_query))
    return back_query, received, done


def attention_weights_kernel(blocks, info, low, mixed, normed, back_query, *refs):
    back_pair = refs[0] if len(refs) == 3 else None
    keep, send = refs[-2:]
    wide = mixed.shape[1]
    size = low.shape[1] // blocks
    parity = lax.rem(info[0], 2)
    for block in range(blocks):
        columns = slice(block * size, (block + 1) * size)
        rows = slice(block // 2 * size, (block // 2 + 1) * size)
        terms = [
            product_left(low[:, columns], mixed[...]).astype(BF16),
            product_left(normed[:, columns], back_query[...]).astype(BF16),
        ]
        if back_pair is not None:
            terms.append(product_left(normed[:, columns], back_pair[...]).astype(BF16))
        terms = jnp.concatenate(terms, axis=1)

        @pl.when(parity == block % 2)
        def _():
            keep[rows, :] = terms

        @pl.when(parity != block % 2)
        def _():
            send[rows, :] = terms


def attention_weights(low, mixed, normed, back_query, back_pair, layout):
    blocks = layout.blocks
    arrays = [low, mixed, normed, back_query] + ([] if back_pair is None else [back_pair])
    total = mixed.shape[1] + sum(array.shape[1] for array in arrays[3:])
    shape = (low.shape[1] // 2, total)
    return call(
        functools.partial(attention_weights_kernel, blocks),
        "attention_weights",
        layout.info,
        arrays,
        [(shape, BF16)] * 2,
    )


def split_kernel(share, *outs):
    start = 0
    for index, out in enumerate(outs):
        turned = index == 0
        size = out.shape[0] if turned else out.shape[1]
        piece = share[:, start : start + size].astype(F32)
        out[...] = piece.T if turned else piece
        start += size


def split_share(share, sizes):
    rows = share.shape[0]
    shapes = [(sizes[0], rows)] + [(rows, size) for size in sizes[1:]]
    return pl.pallas_call(
        split_kernel,
        out_shape=tuple(jax.ShapeDtypeStruct(shape, F32) for shape in shapes),
        in_specs=[WHOLE],
        out_specs=(WHOLE,) * len(shapes),
        compiler_params=pltpu.CompilerParams(vmem_limit_bytes=32 * 1024 * 1024),
        cost_estimate=cost("split_share"),
        name="split_share",
    )(share)


def window(place, part, width):
    return jnp.minimum(place * part // 128 * 128, width - 256)


def cut(scalars, sums, outs):
    @pl.when(pl.program_id(0) == pl.num_programs(0) - 1)
    def _():
        gate, up, down = outs
        size = gate.shape[0]
        rows = pl.ds(pl.multiple_of(scalars[1], 16), size)
        gate[...] = sums[0][rows, :]
        up[...] = sums[1][rows, :]
        down[...] = pltpu.roll(sums[2][...], 256 - scalars[1], 1)[:, :size]


def begin(started, before, outs, first):
    @pl.when(first)
    def _():
        for index, out in enumerate(outs):
            out[...] = before[index][...] if started else jnp.zeros_like(out)


def feedforward_weights_kernel(
    started, scalars, rows, incoming, gate_weight, up_weight, down_weight, *refs
):
    outs = refs[6:9] if started else refs[:3]
    begin(started, refs[:3], outs, pl.program_id(0) == 0)
    gate = product(rows[...], gate_weight[...])
    up = product(rows[...], up_weight[...])
    back_inner = product_right(incoming[...], down_weight[...])
    inner, back_gate, back_up = swiglu_back(gate, up, back_inner)
    columns = pl.ds(pl.multiple_of(scalars[0], 128), 256)
    rows_part, incoming_part = rows[:, columns], incoming[:, columns]
    outs[0][...] += product_left(rows_part, back_gate)
    outs[1][...] += product_left(rows_part, back_up)
    outs[2][...] += product_left(inner, incoming_part)
    if started:
        cut(scalars, outs, refs[3:6])


def feedforward_prepare_kernel(rows, gate_weight, up_weight, inner_out, gate_out, up_out):
    gate = product(rows[...], gate_weight[...])
    up = product(rows[...], up_weight[...])
    chance = 1.0 / (1.0 + jnp.exp(-gate))
    silu = gate * chance
    inner_out[...] = (silu * up).astype(BF16)
    gate_out[...] = (up * (chance + silu * (1.0 - chance))).astype(BF16)
    up_out[...] = silu.astype(BF16)


def feedforward_finish_kernel(
    started, scalars, rows, incoming, inner, gate_slope, up_slope, down_weight, *refs
):
    outs = refs[6:9] if started else refs[:3]
    begin(started, refs[:3], outs, pl.program_id(0) == 0)
    back_inner = product_right(incoming[...], down_weight[...])
    back_gate = (back_inner * gate_slope[...].astype(F32)).astype(BF16)
    back_up = (back_inner * up_slope[...].astype(F32)).astype(BF16)
    columns = pl.ds(pl.multiple_of(scalars[0], 128), 256)
    rows_part, incoming_part = rows[:, columns], incoming[:, columns]
    outs[0][...] += product_left(rows_part, back_gate)
    outs[1][...] += product_left(rows_part, back_up)
    outs[2][...] += product_left(inner[...], incoming_part)
    if started:
        cut(scalars, outs, refs[3:6])


STEP = 256


def fixed(shape):
    return pl.BlockSpec(shape, lambda i: (0,) * len(shape), pipeline_mode=pl.Buffered(1))


def moving(columns, offset=0):
    return pl.BlockSpec((STEP, columns), lambda i: (i + offset, 0))


def weight_call(kernel, name, layout, moved, still, hidden, steps, before):
    width = moved[0][1][-1]
    shapes = [(256, hidden), (256, hidden), (hidden, 256)]
    started = before is not None
    earlier = list(before) if started else []
    kept = lambda shape: pl.BlockSpec(
        shape, lambda i, s: (0,) * len(shape), pipeline_mode=pl.Buffered(1)
    )
    size = width // layout.blocks
    own = window(layout.own, size, width)
    place = jnp.stack([own, layout.own * size - own])
    outs = [(size, hidden), (size, hidden), (hidden, size)] if started else shapes
    return pl.pallas_call(
        functools.partial(kernel, started),
        out_shape=tuple(jax.ShapeDtypeStruct(shape, F32) for shape in outs),
        grid_spec=pltpu.PrefetchScalarGridSpec(
            num_scalar_prefetch=1,
            grid=(steps,),
            in_specs=[pl.BlockSpec(block, place) for _, block, place in moved]
            + [kept(array.shape) for array in still]
            + ([kept(shape) for shape in shapes] if started else []),
            out_specs=tuple(kept(shape) for shape in outs),
            scratch_shapes=[pltpu.VMEM(shape, F32) for shape in shapes] if started else [],
        ),
        compiler_params=pltpu.CompilerParams(vmem_limit_bytes=48 * MEGA),
        cost_estimate=cost(name),
        name=name,
    )(place, *[array for array, _, _ in moved], *still, *earlier)


def feedforward_weights(rows, incoming, weights, layout, before):
    total, width = rows.shape
    steps = total // STEP
    moved = [
        (rows, (STEP, width), lambda i, s: (i, 0)),
        (incoming, (STEP, width), lambda i, s: (i, 1)),
    ]
    return weight_call(
        feedforward_weights_kernel,
        "feedforward_weights",
        layout,
        moved,
        weights[6:9],
        weights[6].shape[1],
        steps,
        before,
    )


def feedforward_finish(rows, incoming, prepared, weights, layout, before):
    width = weights[6].shape[0]
    moved = [
        (array, (STEP, min(width, array.shape[1])), lambda i, s: (i, 0))
        for array in (rows, incoming, *prepared)
    ]
    return weight_call(
        feedforward_finish_kernel,
        "feedforward_finish",
        layout,
        moved,
        weights[8:9],
        weights[6].shape[1],
        rows.shape[0] // STEP,
        before,
    )


def feedforward_prepare(rows, weights):
    total, width = rows.shape[0], weights[6].shape[0]
    hidden = weights[6].shape[1]
    return pl.pallas_call(
        feedforward_prepare_kernel,
        grid=(total // STEP,),
        out_shape=(jax.ShapeDtypeStruct((total, hidden), BF16),) * 3,
        in_specs=[moving(width), fixed((width, hidden)), fixed((width, hidden))],
        out_specs=(moving(hidden),) * 3,
        compiler_params=pltpu.CompilerParams(vmem_limit_bytes=48 * 1024 * 1024),
        cost_estimate=cost("feedforward_prepare"),
        name="feedforward_prepare",
    )(rows, weights[6], weights[7])


def swiglu_back(gate, up, back_inner):
    chance = 1.0 / (1.0 + jnp.exp(-gate))
    silu = gate * chance
    inner = (silu * up).astype(BF16)
    back_gate = (back_inner * up * (chance + silu * (1.0 - chance))).astype(BF16)
    back_up = (back_inner * silu).astype(BF16)
    return inner, back_gate, back_up


class Layout:
    def __init__(self, lengths, tokens):
        self.tokens = tokens
        self.blocks = lax.axis_size("blk")
        self.own = lax.axis_index("blk")
        self.core = lax.rem(lax.axis_index("tp"), 2)
        index = jnp.arange(tokens * self.blocks, dtype=jnp.int32)
        firsts = first_tokens(lengths, index)
        mine = lax.dynamic_slice_in_dim(index - firsts, self.own * tokens, tokens, 0)
        self.tables = rotary_tables(mine)
        self.firsts = firsts.reshape(self.blocks, tokens)
        self.info = jnp.stack([self.own, self.core]).astype(jnp.int32)


def attention_share(normed, back_rows, blocks):
    return sum_blocks(product_left(normed, back_rows).astype(BF16), blocks)


def body(tokens, lengths, *rest):
    one, two, cotangent = rest[:9], rest[9:18], rest[18]
    layout = Layout(lengths, tokens.shape[0])
    core, blocks = layout.core, layout.blocks
    heads = one[2].shape[1] // HEAD_SIZE
    group = one[1].shape[1] // HEAD_SIZE // heads

    wide, narrow = one[1].shape[1], one[2].shape[1]

    normed_one, query_one, pair_one = front(tokens, None, one, layout)
    pairs_one = gather_pairs(pair_one, blocks)
    mixed_one, logs_one, send, keep = attend(query_one, pairs_one, one[4], layout, heads, group)
    hidden_one, inner_in_one, half_one, send, keep = feed_forward(
        tokens, sum_tp(send, keep), cotangent, one, layout
    )
    pieces = sum_tp(send, keep)
    rows_one = gather_rows(half_one)

    normed_two, query_two, pair_two, inputs_two = front(hidden_one, pieces, two, layout)
    pairs_two = gather_pairs(pair_two, blocks)
    mixed_two, logs_two, send, keep = attend(query_two, pairs_two, two[4], layout, heads, group)

    def prepare(rows, after):
        return feedforward_prepare(tie(after, rows)[1], one)

    pieces = sum_tp(send, keep)

    hidden_two, half_two, last_send, last_keep, send, keep = feed_both(
        inputs_two, pieces, cotangent, two, layout
    )
    rows_two = gather_rows(half_two)

    pieces = sum_tp(send, keep)
    back_hidden, low, back_mixed, delta, gain_feed_two = middle_back(
        hidden_two, cotangent, pieces, two, mixed_two, layout
    )

    def finish_forward(after):
        whole, other = sum_tp(tie(after, last_send)[1], last_keep)
        top, bottom = jnp.where(core == 0, whole, other), jnp.where(core == 0, other, whole)
        last = jnp.concatenate([top, bottom], axis=0).astype(F32)
        return (hidden_two + last).astype(BF16), prepare(rows_one[0], after)

    back_query, received, (result, prepared_own) = attention_back(
        query_two, back_mixed, logs_two, delta, pairs_two, layout, heads, group, finish_forward
    )
    back_pair, send, keep = pair_back(received, back_query, two, layout)

    state = [None]
    early = [None]

    def weights_two(piece):
        rows, incoming = early[0][piece], rows_one[piece]

        def run(after):
            held, rows_now, incoming_now = tie(after, rows, incoming)
            state[0] = feedforward_weights(
                rows_now, incoming_now, two, layout, state[0]
            )
            return state[0]

        return run

    terms_two = (low, mixed_two, normed_two, back_query, back_pair)

    def share_second(after):
        terms = tie(after, *terms_two)[1:]
        return attention_weights(*terms, layout)

    pieces, bucket_two = sum_tp(send, keep, share_second)

    gradient, half_low, gain_attention_two, send, keep = feed_back(
        inputs_two, two[0], back_hidden, pieces, inner_in_one, one, layout
    )

    pieces, prepared_other = sum_tp(send, keep, lambda after: prepare(rows_one[1], after))
    half_low, pieces = tie(half_low, pieces)
    early[0] = rows_two
    ends = gather_rows(half_low)
    share_two = scatter_blocks(sum_pair(*bucket_two, blocks), blocks)
    back_hidden, low, back_mixed, delta, gain_feed_one = middle_back(
        hidden_one, gradient, pieces, one, mixed_one, layout
    )
    back_query, received, state[0] = attention_back(
        query_one, back_mixed, logs_one, delta, pairs_one, layout, heads, group, weights_two(0)
    )
    back_pair, send, keep = pair_back(received, back_query, one, layout)

    def share_first(after):
        terms = tie(after, low, mixed_one, normed_one, back_query)[1:]
        return attention_weights(*terms, None, layout), weights_two(1)(after)

    pieces, (bucket_one, state[0]) = sum_tp(send, keep, share_first)
    share_one = scatter_blocks(sum_pair(*bucket_one, blocks), blocks)
    tokens_gradient, gain_attention_one = inputs_back(tokens, one[0], back_hidden, pieces, layout)
    feed_two = state[0]
    feed_one = None
    for rows, end, prepared in zip(rows_one, ends, (prepared_own, prepared_other)):
        feed_one = feedforward_finish(rows, end, prepared, one, layout, feed_one)
    share_pair_one = attention_share(normed_one, back_pair, blocks)
    projection_two, *others_two = split_share(share_two, (wide, wide, narrow, narrow))
    projection_one, gradient_query_one = split_share(share_one, (wide, wide))
    shares_two = (*others_two, projection_two)
    shares_one = (
        gradient_query_one,
        share_pair_one[:, :narrow],
        share_pair_one[:, narrow:],
        projection_one,
    )
    gains = jnp.stack([gain_attention_one, gain_feed_one, gain_attention_two, gain_feed_two])
    gains, feed_one = tie(gains, tuple(feed_one))
    gains = gains.reshape(4, blocks, -1).transpose(1, 0, 2)
    gains = jnp.sum(lax.all_to_all(gains, "blk", 0, 0, tiled=True), axis=0)
    return (
        (result, tokens_gradient)
        + (gains[0],)
        + shares_one
        + (gains[1],)
        + tuple(feed_one)
        + (gains[2],)
        + shares_two
        + (gains[3],)
        + tuple(feed_two)
    )


def solution(mesh):
    rows, columns = P("tp", None), P(None, "tp")
    layer = (P(), columns, columns, columns, rows, P(), columns, columns, rows)
    in_specs = (P("blk", None), P()) + layer + layer + (P("blk", None),)
    wide_out, tall_out = P("blk", "tp"), P("tp", "blk")
    layer_out = (
        P("blk"),
        wide_out,
        wide_out,
        wide_out,
        tall_out,
        P("blk"),
        wide_out,
        wide_out,
        tall_out,
    )
    out_specs = (P("blk", None), P("blk", None)) + layer_out + layer_out
    return jax.shard_map(body, mesh=mesh, in_specs=in_specs, out_specs=out_specs, check_vma=False)
```
